32 devices in a mesh: slices: 2 (over y), modes: 4 (over z), half: 4 (over x, core).
Axes of the slice: x: 2, y: 2, z: 4, core: 2. Of those that a mesh axis runs over, the one named last changes fastest.
Arguments:
- stem_state: bfloat16 [2, 8, 4, 2, 128, 128], P(None, ('slices', 'modes'), 'half'), parts along dimension 1, may hold values from -6 to 6
- branch_mats: bfloat16 [4, 6, 2, 128, 128], replicated, may hold values from -1 to 1
- branch_modes: int32 [4, 6], replicated, may hold values from 0 to 1
- out_proj: bfloat16 [4, 2, 512, 256], P('half'), may hold values from -0.1875 to 0.1875
- groups: int32 [8, 4, 64, 1], P(('slices', 'modes'), 'half'), parts along dimension 0, may hold values from 0 to 3; in each aligned block of 64 rows (0 to 63, 64 to 127, ..., all dimensions but the last counted through in order) at most 16 rows name the same one
Outputs:
- amplitudes: bfloat16 [8, 4, 2, 64, 256], P(('slices', 'modes'), 'half'), parts along dimension 0
The draws below stay inside these ranges and needn't reach their ends.
There are 2 independent parts, one for each index of `slices`. The reference program is written for one: setup_inputs(seed, part) draws one part's arguments, and reference() takes and returns one part's arrays. A program takes and returns all parts, laid end to end along the dimension named above; an argument that names none is the same for every part. Nothing has to cross between parts.
Inputs may be any that keep to these rules, and one draw needn't show every extreme that they name: `branch_modes`: 0: the branch contracts the fifth index b of the state, 1: the sixth index c. `groups`: the 64 rows of one device name one group at most 16 times, and some device names some group exactly 16 times.
All inputs are finite; a program needn't handle non-finite values.
Results may differ from the reference program's by a relative error of at most 0.025.
Values may be sent and summed in bfloat16 or wider, within the bound.
A program may use at most 64 MiB of HBM per device.

```python
import math
import jax
import jax.numpy as jnp
import numpy as np
from jax import lax

BRANCH = 128
STEM = 512
OUT_WIDTH = 256
LEGS = 4
BRANCHES = 6
SLABS = 2
ROWS_DEV = 64
CAPACITY = 16
N_MODES = 4
N_HALF = 4


def draw_branch_mats(key, part):
    base = jax.random.fold_in(key, 7)
    key_angle = jax.random.fold_in(base, 1)
    key_real = jax.random.fold_in(base, 2)
    key_imag = jax.random.fold_in(base, 3)
    angles = jax.random.uniform(key_angle, (LEGS, BRANCHES, BRANCH), jnp.float32, -math.pi, math.pi)
    sigma = 0.25 / math.sqrt(2.0 * BRANCH)
    shape = (LEGS, BRANCHES, BRANCH, BRANCH)
    noise_real = jax.random.normal(key_real, shape, jnp.float32) * sigma
    noise_imag = jax.random.normal(key_imag, shape, jnp.float32) * sigma
    identity = jnp.eye(BRANCH, dtype=jnp.float32)
    offdiag = 1.0 - identity
    diag_real = identity * jnp.cos(angles)[..., :, None]
    diag_imag = identity * jnp.sin(angles)[..., :, None]
    factor = 1.0 / math.sqrt(1.0625)
    real_part = (diag_real + noise_real * offdiag) * factor
    imag_part = (diag_imag + noise_imag * offdiag) * factor
    stacked = jnp.stack([real_part, imag_part], axis=2)
    return jnp.clip(stacked, -1.0, 1.0).astype(jnp.bfloat16)


def touch_ends(drawn, stream_key, low, high):
    place = [jax.random.randint(jax.random.fold_in(stream_key, axis), (), 0, length) for axis, length in enumerate(drawn.shape)]
    main_axis = drawn.shape.index(max(drawn.shape))
    next_to = place[:main_axis] + [(place[main_axis] + 1) % drawn.shape[main_axis]] + place[main_axis + 1:]
    return drawn.at[tuple(place)].set(low).at[tuple(next_to)].set(high)


def block_scale(stream_key, shape, split, smallest, top_value):
    gain, own = 1.0, jax.random.fold_in(stream_key, 6)
    for position, parts in split:
        heights = jnp.exp(jax.random.uniform(jax.random.fold_in(own, position), (parts,), jnp.float32, smallest / len(split), top_value / len(split)))
        gain = gain * jnp.repeat(heights, shape[position] // parts).reshape([-1 if axis == position else 1 for axis in range(len(shape))])
    return gain


def shared_out(own_key, own, number, rows, count, top, reach, skew):
    order = jax.random.permutation(own_key, count)
    crowded, common = load_shares(count, rows * top, reach, skew, True), load_shares(count, rows * top, reach, skew, False)
    places = jnp.arange(count)

    def named(lengths, rotation):
        used = int((lengths > 0).sum())
        fixed = max(1, used // 4)
        moved = fixed + (places - fixed + rotation * (used - fixed)) % max(1, count - fixed)
        return jnp.zeros((count,), jnp.int32).at[order[jnp.where(places < fixed, places, moved)]].set(jnp.asarray(lengths, jnp.int32))

    lengths = jnp.where(number % 4 == 0, named(crowded, number // 4), named(common, number - number // 4 - 1))
    mixed = jax.random.permutation(jax.random.fold_in(own, 3), count)
    giver, taker = mixed[0:count // 2 * 2:2], mixed[1:count // 2 * 2:2]
    slack = jnp.minimum(lengths[giver] - 1, reach - lengths[taker]) // 2
    slack = jnp.where((giver == order[0]) | (taker == order[0]) | (lengths[taker] == 0), 0, jnp.maximum(slack, 0))
    moved = jax.random.randint(jax.random.fold_in(own, 4), (count // 2,), 0, 1 << 20) % (slack + 1)
    lengths = lengths.at[giver].add(-moved).at[taker].add(moved)
    members = jnp.searchsorted(jnp.cumsum(lengths), jnp.arange(rows * top), side="right").astype(jnp.int32)
    table = members.reshape(top, rows).T
    table = table[jax.random.permutation(jax.random.fold_in(own, 1), rows)]
    rotation = jax.random.randint(jax.random.fold_in(own, 2), (rows, 1), 0, top)
    return jnp.take_along_axis(table, (jnp.arange(top)[None, :] + rotation) % top, axis=1)


def load_shares(amount, total, limit, slope, full):
    weights = [(1 << 20) // math.isqrt(grade ** slope) + 1 for grade in range(1, amount + 1)]
    largest = limit if full else min(limit, max(-(-total // amount), total * weights[0] // sum(weights)))
    least = 1 if total - largest >= amount - 1 else 0
    given, spare = [largest] + [least] * (amount - 1), total - largest - least * (amount - 1)
    while spare > 0:
        candidates = [i for i in range(1, amount) if given[i] < largest] or [i for i in range(1, amount) if given[i] < limit]
        pool, left = sum([weights[i] for i in candidates]), spare
        for i in candidates:
            extra = min(limit - given[i], max(1, left * weights[i] // pool), spare)
            given[i] = given[i] + extra
            spare = spare - extra
    return np.array(given)


def normal_values(stream_key, extent, width, limit, split=(), kind=jnp.bfloat16):
    gain = block_scale(stream_key, extent, split, -0.22, 0.18) if split else 1.0
    drawn = jax.random.normal(stream_key, extent, jnp.float32) * width * gain
    return jnp.minimum(jnp.maximum(drawn, -limit), limit).astype(kind)


def setup_inputs(seed: int = 0, part: int = 0) -> dict:
    keys = jax.random.split(jax.random.key(seed), 6)
    part_splits = jax.random.split(jax.random.fold_in(keys[5], part), 6)
    stem_state = normal_values(part_splits[0], (2, N_MODES, N_HALF, SLABS, BRANCH, BRANCH), 1.0, 6.0, ((1, 4), (2, 4)))
    branch_mats = draw_branch_mats(jax.random.fold_in(keys[5], 71), part)
    branch_modes = touch_ends(jax.random.randint(keys[2], (LEGS, BRANCHES), 0, 2), jax.random.fold_in(keys[2], 1), 0, 1).astype(jnp.int32)
    out_proj = normal_values(keys[3], (N_HALF, 2, STEM, OUT_WIDTH), (2 * STEM) ** -0.5, 0.1875, ((0, 4),))
    groups_keys = jax.random.split(jax.random.fold_in(part_splits[4], 1), N_MODES * N_HALF * ROWS_DEV // ROWS_DEV)
    groups_turns = jax.random.permutation(jax.random.fold_in(part_splits[4], 3), N_MODES * N_HALF * ROWS_DEV // ROWS_DEV)
    groups = jax.vmap(lambda own, number: shared_out(jax.random.fold_in(part_splits[4], 2), own, number, ROWS_DEV, N_HALF, 1, CAPACITY, 2))(groups_keys, groups_turns).reshape((N_MODES, N_HALF, ROWS_DEV, 1))
    return dict(stem_state=stem_state, branch_mats=branch_mats, branch_modes=branch_modes, out_proj=out_proj, groups=groups)


def widen(matrix):
    real_part = matrix[0]
    imag_part = matrix[1]
    return jnp.stack([jnp.stack([real_part, imag_part]), jnp.stack([-imag_part, real_part])])


def contract_first(state, wide):
    value = jnp.einsum('imhsbc,ijbd->jmhsdc', state.astype(jnp.float32), wide.astype(jnp.float32), precision=lax.Precision.HIGHEST)
    return value.astype(jnp.bfloat16)


def contract_second(state, wide):
    value = jnp.einsum('imhsbc,ijcd->jmhsbd', state.astype(jnp.float32), wide.astype(jnp.float32), precision=lax.Precision.HIGHEST)
    return value.astype(jnp.bfloat16)


def swap_modes(state):
    comps, nmodes, nhalf, slabs, inner, outer = state.shape
    spread = state.reshape(comps, nmodes, nhalf, slabs, inner, nmodes, outer // nmodes)
    spread = jnp.swapaxes(spread, 1, 5)
    return spread.reshape(comps, nmodes, nhalf, slabs, inner, outer)


def reference(stem_state, branch_mats, branch_modes, out_proj, groups):
    state = stem_state
    for leg in range(LEGS):
        for branch in range(BRANCHES):
            wide = widen(branch_mats[leg, branch])
            state = lax.cond(branch_modes[leg, branch] == 0, contract_first, contract_second, state, wide)
        state = swap_modes(state)
    comps, nmodes, nhalf = state.shape[0], state.shape[1], state.shape[2]
    rows = state.reshape(comps, nmodes, nhalf, ROWS_DEV, STEM).astype(jnp.float32)
    chosen = groups[..., 0]
    result = jnp.zeros((2, nmodes, nhalf, ROWS_DEV, OUT_WIDTH), jnp.float32)
    for owner in range(N_HALF):
        wide = widen(out_proj[owner]).astype(jnp.float32)
        product = jnp.einsum('imhrk,ijkd->jmhrd', rows, wide, precision=lax.Precision.HIGHEST)
        result = jnp.where((chosen == owner)[None, :, :, :, None], product, result)
    return jnp.transpose(result, (1, 2, 0, 3, 4)).astype(jnp.bfloat16)
```

```python
import functools

import jax
import jax.numpy as jnp
from jax import lax
from jax.experimental import pallas as pl
from jax.experimental.pallas import tpu as pltpu
from jax.sharding import PartitionSpec as P

MESH = pl.DeviceIdType.MESH
CHUNKS = 4


def widen(matrix):
    real_part = matrix[0]
    imag_part = matrix[1]
    return jnp.stack([jnp.stack([real_part, imag_part]), jnp.stack([-imag_part, real_part])])


def contract_first(state, wide):
    value = jnp.einsum("isbc,ijbd->jsdc", state, wide, preferred_element_type=jnp.float32)
    return value.astype(jnp.bfloat16)


def contract_second(state, wide):
    value = jnp.einsum("isbc,ijcd->jsbd", state, wide, preferred_element_type=jnp.float32)
    return value.astype(jnp.bfloat16)


def stepwise(stem_state, branch_mats, branch_modes, out_proj, groups):
    slabs = stem_state.shape[3]
    inner = stem_state.shape[4]
    state = stem_state.reshape(2, slabs, inner, inner)
    peers = lax.axis_size("modes")
    width_part = inner // peers
    for leg in range(branch_mats.shape[0]):

        def advance(branch, current):
            wide = widen(branch_mats[leg][branch])
            return lax.cond(
                branch_modes[leg][branch] == 0, contract_first, contract_second, current, wide
            )

        state = lax.fori_loop(0, branch_mats.shape[1], advance, state)
        pieces = state.reshape(2, slabs, inner, peers, width_part)
        pieces = jnp.transpose(pieces, (3, 0, 1, 2, 4)).reshape(peers, 2, slabs, inner * width_part)
        pieces = lax.all_to_all(pieces, "modes", split_axis=0, concat_axis=0, tiled=True)
        pieces = pieces.reshape(peers, 2, slabs, inner, width_part)
        state = jnp.transpose(pieces, (1, 2, 3, 0, 4)).reshape(2, slabs, inner, inner)
    stem_len = out_proj.shape[2]
    out_len = out_proj.shape[3]
    row_total = slabs * inner * inner // stem_len
    rows = state.reshape(2, row_total, stem_len)
    chosen = groups.reshape(row_total)
    piece = lax.all_gather(out_proj, "half", axis=0, tiled=True)
    wides = jax.vmap(widen)(piece)
    product = jnp.einsum("irk,gijkd->gjrd", rows, wides, preferred_element_type=jnp.float32)
    owners = jnp.arange(piece.shape[0], dtype=jnp.int32)
    keep = chosen[None, :] == owners[:, None]
    products = jnp.where(keep[:, None, :, None], product, 0.0)
    result = jnp.sum(products, axis=0).astype(jnp.bfloat16)
    return result.reshape(1, 1, 2, row_total, out_len)


def dot(left, right):
    return jnp.dot(left, right, preferred_element_type=jnp.float32)


def wide_of(top):
    inner = top.shape[0]
    real_part, imag_part = top[:, :inner], top[:, inner:]
    return jnp.concatenate([top, jnp.concatenate([-imag_part, real_part], axis=1)], axis=0)


def normal(top):
    largest = jnp.max(jnp.abs(top), axis=(0, 1), keepdims=True)
    largest = jnp.where(largest > 0.0, largest, 1.0)
    return top / largest, largest


def fused(
    sizes,
    state_ref,
    mats_hbm,
    modes_ref,
    proj_ref,
    groups_ref,
    out_ref,
    mats,
    got,
    leave,
    back,
    weights,
    local_sem,
    first_send,
    first_recv,
    last_send,
    last_recv,
    x_send,
    x_recv,
    y_send,
    y_recv,
    core_send,
    core_recv,
):
    peers, legs, branches, slabs, inner, depth = sizes
    width = inner // peers
    me = lax.axis_index("modes")
    row = lax.axis_index("slices")
    home = lax.axis_index("half")
    core = lax.rem(home, 2)
    sibling = home + 1 - 2 * core
    across = lax.rem(home + 2, 4)
    across_sibling = lax.rem(sibling + 2, 4)
    other_row = 1 - row
    part = got.shape[2]
    half_depth = depth // 2
    piece = half_depth // CHUNKS

    load_mats = pltpu.make_async_copy(mats_hbm, mats, local_sem.at[0])
    load_mats.start()
    load_own = pltpu.make_async_copy(
        state_ref.at[:, pl.ds(me * part, part), :], got.at[me], local_sem.at[1]
    )
    load_own.start()
    load_proj = pltpu.make_async_copy(proj_ref, weights.at[home], local_sem.at[2])
    load_proj.start()

    barrier = pltpu.get_barrier_semaphore()
    for step in range(1, peers):
        pl.semaphore_signal(
            barrier, inc=1, device_id={"modes": lax.rem(me + step, peers)}, device_id_type=MESH
        )
    pl.semaphore_signal(barrier, inc=1, device_id={"half": sibling}, device_id_type=MESH)
    pl.semaphore_signal(barrier, inc=1, device_id={"half": across}, device_id_type=MESH)
    pl.semaphore_signal(barrier, inc=1, device_id={"slices": other_row}, device_id_type=MESH)
    pl.semaphore_wait(barrier, peers + 2)

    first = []
    for step in range(1, peers):
        target = lax.rem(me + step, peers)
        copy = pltpu.make_async_remote_copy(
            src_ref=state_ref.at[:, pl.ds(target * part, part), :],
            dst_ref=got.at[me],
            send_sem=first_send.at[step - 1],
            recv_sem=first_recv.at[step - 1],
            device_id={"modes": target},
            device_id_type=MESH,
        )
        copy.start()
        first.append(copy)

    def rows_of(which, chunk):
        return pl.ds(which * half_depth + chunk * piece, piece)

    over_x, over_y, over_core = [], [], []
    for chunk in range(CHUNKS):
        copy = pltpu.make_async_remote_copy(
            src_ref=proj_ref.at[:, rows_of(row, chunk), :],
            dst_ref=weights.at[home, :, rows_of(row, chunk), :],
            send_sem=x_send.at[chunk],
            recv_sem=x_recv.at[chunk],
            device_id={"half": across},
            device_id_type=MESH,
        )
        copy.start()
        over_x.append(copy)
    own = pltpu.make_async_remote_copy(
        src_ref=proj_ref,
        dst_ref=weights.at[home],
        send_sem=core_send.at[0],
        recv_sem=core_recv.at[0],
        device_id={"half": sibling},
        device_id_type=MESH,
    )
    own.start()

    def to_core(which, chunk, number):
        copy = pltpu.make_async_remote_copy(
            src_ref=weights.at[across, :, rows_of(which, chunk), :],
            dst_ref=weights.at[across, :, rows_of(which, chunk), :],
            send_sem=core_send.at[number],
            recv_sem=core_recv.at[number],
            device_id={"half": sibling},
            device_id_type=MESH,
        )
        copy.start()
        over_core.append(copy)

    def hand_on(chunk):
        over_x[chunk].wait_recv()
        copy = pltpu.make_async_remote_copy(
            src_ref=weights.at[across, :, rows_of(row, chunk), :],
            dst_ref=weights.at[across, :, rows_of(row, chunk), :],
            send_sem=y_send.at[chunk],
            recv_sem=y_recv.at[chunk],
            device_id={"slices": other_row},
            device_id_type=MESH,
        )
        copy.start()
        over_y.append(copy)
        to_core(row, chunk, 1 + chunk)

    def take_in(chunk):
        over_y[chunk].wait_recv()
        to_core(other_row, chunk, 1 + CHUNKS + chunk)

    load_mats.wait()
    lanes = lax.broadcasted_iota(jnp.int32, (inner, 2 * inner), 1)
    sublanes = lax.broadcasted_iota(jnp.int32, (inner, 2 * inner), 0)
    identity = jnp.where(lanes == sublanes, 1.0, 0.0).astype(jnp.float32)
    over_b, over_c = [], []
    for leg in range(legs):
        top = jnp.concatenate([mats[leg, 0, 0], mats[leg, 0, 1]], axis=1).astype(jnp.float32)
        is_b = modes_ref[leg, 0] == 0
        over_b.append(jnp.where(is_b, top, identity))
        over_c.append(jnp.where(is_b, identity, top))
    for branch in range(1, branches):
        for leg in range(legs):
            is_b = modes_ref[leg, branch] == 0
            top = jnp.concatenate([mats[leg, branch, 0], mats[leg, branch, 1]], axis=1)
            chosen = jnp.where(is_b, over_b[leg], over_c[leg]).astype(jnp.bfloat16)
            value = dot(chosen, wide_of(top))
            over_b[leg] = jnp.where(is_b, value, over_b[leg])
            over_c[leg] = jnp.where(is_b, over_c[leg], value)
    gains = []
    wides = []
    for leg in range(legs):
        scaled, gain = normal(over_c[leg])
        gains.append(gain)
        wides.append(wide_of(scaled.astype(jnp.bfloat16)))
        scaled, gain = normal(over_b[leg])
        gains.append(gain)
        over_b[leg] = scaled.astype(jnp.bfloat16)

    load_own.wait()
    for copy in first:
        copy.wait()
    values = jnp.concatenate(
        [jnp.concatenate([got[m, 0], got[m, 1]], axis=1) for m in range(peers)], axis=0
    )
    block = lax.broadcasted_iota(jnp.int32, (part, inner), 1) // width
    for leg in range(legs):
        product = dot(values, wides[leg])
        swapped = []
        for m in range(peers):
            both = []
            for comp in range(2):
                taken = None
                for t in range(peers):
                    tile = product[t * part : (t + 1) * part, comp * inner : (comp + 1) * inner]
                    shift = (t - m) * width % inner
                    if shift:
                        tile = pltpu.roll(tile, shift, 1)
                    taken = tile if taken is None else jnp.where(block == t, tile, taken)
                both.append(taken)
            swapped.append(jnp.concatenate(both, axis=1))
        values = jnp.concatenate(swapped, axis=0).astype(jnp.bfloat16)
    for m in range(peers):
        leave[m] = values[m * part : (m + 1) * part]

    last = []
    for step in range(1, peers):
        target = lax.rem(me + step, peers)
        copy = pltpu.make_async_remote_copy(
            src_ref=leave.at[target],
            dst_ref=back.at[me],
            send_sem=last_send.at[step - 1],
            recv_sem=last_recv.at[step - 1],
            device_id={"modes": target},
            device_id_type=MESH,
        )
        copy.start()
        last.append(copy)
    back[me] = leave[me]
    for chunk in range(CHUNKS):
        hand_on(chunk)

    total = over_b[0]
    for leg in range(1, legs):
        total = dot(total, wide_of(over_b[leg])).astype(jnp.bfloat16)
    stacked = jnp.concatenate([total[:, :inner], total[:, inner:]], axis=0)
    quad = depth // inner
    short = inner // quad
    target_row = lax.broadcasted_iota(jnp.int32, (inner, inner), 0)
    source_col = lax.broadcasted_iota(jnp.int32, (inner, inner), 1)
    order = (source_col % quad) * short + source_col // quad == target_row
    order = jnp.where(order, 1.0, 0.0).astype(jnp.bfloat16)
    turned = lax.dot_general(
        order, stacked, (((1,), (1,)), ((), ())), preferred_element_type=jnp.float32
    ).astype(jnp.bfloat16)
    real_part, imag_part = turned[:, :inner], turned[:, inner:]
    left = jnp.concatenate(
        [
            jnp.concatenate([real_part, -imag_part], axis=1),
            jnp.concatenate([imag_part, real_part], axis=1),
        ],
        axis=0,
    )
    for chunk in range(CHUNKS):
        take_in(chunk)

    for copy in last:
        copy.wait()
    arrived = jnp.concatenate([back[m] for m in range(peers)], axis=0)
    right = jnp.concatenate(
        [
            jnp.concatenate(
                [
                    arrived[s * inner : (s + 1) * inner, comp * inner : (comp + 1) * inner]
                    for s in range(slabs)
                ],
                axis=1,
            )
            for comp in range(2)
        ],
        axis=0,
    )
    final = dot(left, right).astype(jnp.bfloat16)
    rows = jnp.concatenate(
        [
            jnp.concatenate(
                [
                    final[
                        comp * inner + q * short : comp * inner + (q + 1) * short,
                        s * inner : (s + 1) * inner,
                    ]
                    for q in range(quad)
                ],
                axis=1,
            )
            for comp in range(2)
            for s in range(slabs)
        ],
        axis=0,
    )
    count = slabs * short
    named = groups_ref[...]
    real_sum = jnp.zeros(out_ref.shape[1:], jnp.float32)
    imag_sum = jnp.zeros(out_ref.shape[1:], jnp.float32)

    def project(group, real_sum, imag_sum):
        by_real = dot(rows, weights[group, 0])
        by_imag = dot(rows, weights[group, 1])
        here = named == group
        real_sum = jnp.where(here, by_real[:count] - by_imag[count:], real_sum)
        imag_sum = jnp.where(here, by_imag[:count] + by_real[count:], imag_sum)
        return real_sum, imag_sum

    load_proj.wait()
    real_sum, imag_sum = project(home, real_sum, imag_sum)
    own.wait()
    real_sum, imag_sum = project(sibling, real_sum, imag_sum)
    real_sum, imag_sum = project(across, real_sum, imag_sum)
    for copy in over_core:
        copy.wait()
    real_sum, imag_sum = project(across_sibling, real_sum, imag_sum)
    for gain in [jnp.minimum(g, 1.0) for g in gains] + [jnp.maximum(g, 1.0) for g in gains]:
        real_sum = real_sum * gain
        imag_sum = imag_sum * gain
    out_ref[0] = real_sum.astype(jnp.bfloat16)
    out_ref[1] = imag_sum.astype(jnp.bfloat16)
    for copy in over_x:
        copy.wait_send()
    for copy in over_y:
        copy.wait_send()


def local(stem_state, branch_mats, branch_modes, out_proj, groups):
    slabs, inner = stem_state.shape[3], stem_state.shape[4]
    legs, branches = branch_mats.shape[:2]
    depth, out_len = out_proj.shape[2:]
    peers = lax.axis_size("modes")
    rows = slabs * inner
    row_total = rows * inner // depth
    part = rows // peers
    bf16 = jnp.bfloat16
    whole = pl.BlockSpec(memory_space=pl.ANY)
    result = pl.pallas_call(
        functools.partial(fused, (peers, legs, branches, slabs, inner, depth)),
        out_shape=jax.ShapeDtypeStruct((2, row_total, out_len), bf16),
        in_specs=[
            whole,
            whole,
            pl.BlockSpec(memory_space=pltpu.SMEM),
            whole,
            pl.BlockSpec(memory_space=pltpu.VMEM),
        ],
        out_specs=pl.BlockSpec(memory_space=pltpu.VMEM),
        scratch_shapes=[
            pltpu.VMEM(branch_mats.shape, bf16),
            pltpu.VMEM((peers, 2, part, inner), bf16),
            pltpu.VMEM((peers, part, 2 * inner), bf16),
            pltpu.VMEM((peers, part, 2 * inner), bf16),
            pltpu.VMEM((lax.axis_size("half"), 2, depth, out_len), bf16),
            pltpu.SemaphoreType.DMA((3,)),
            pltpu.SemaphoreType.DMA((peers - 1,)),
            pltpu.SemaphoreType.DMA((peers - 1,)),
            pltpu.SemaphoreType.DMA((peers - 1,)),
            pltpu.SemaphoreType.DMA((peers - 1,)),
            pltpu.SemaphoreType.DMA((CHUNKS,)),
            pltpu.SemaphoreType.DMA((CHUNKS,)),
            pltpu.SemaphoreType.DMA((CHUNKS,)),
            pltpu.SemaphoreType.DMA((CHUNKS,)),
            pltpu.SemaphoreType.DMA((1 + 2 * CHUNKS,)),
            pltpu.SemaphoreType.DMA((1 + 2 * CHUNKS,)),
        ],
        compiler_params=pltpu.CompilerParams(
            collective_id=0, has_side_effects=True, vmem_limit_bytes=40 * 1024 * 1024
        ),
    )(
        stem_state.reshape(2, rows, inner),
        branch_mats,
        branch_modes,
        out_proj.reshape(out_proj.shape[1:]),
        groups.reshape(row_total, 1),
    )
    return result.reshape(1, 1, 2, row_total, out_len)


def solution(mesh):
    placed = (
        P(None, ("slices", "modes"), "half", None, None, None),
        P(),
        P(),
        P("half", None, None, None),
        P(("slices", "modes"), "half", None, None),
    )
    sizes = dict(mesh.shape)
    in_kernel = sizes["half"] == 4 and sizes["slices"] == 2 and sizes["modes"] <= 4
    return jax.shard_map(
        local if in_kernel else stepwise,
        mesh=mesh,
        in_specs=placed,
        out_specs=P(("slices", "modes"), "half", None, None, None),
        check_vma=False,
    )
```

```python
import functools

import jax
import jax.numpy as jnp
from jax import lax
from jax.experimental import pallas as pl
from jax.experimental.pallas import tpu as pltpu
from jax.sharding import PartitionSpec as P

MESH = pl.DeviceIdType.MESH
CHUNKS = 4


def widen(matrix):
    real_part = matrix[0]
    imag_part = matrix[1]
    return jnp.stack([jnp.stack([real_part, imag_part]), jnp.stack([-imag_part, real_part])])


def contract_first(state, wide):
    value = jnp.einsum("isbc,ijbd->jsdc", state, wide, preferred_element_type=jnp.float32)
    return value.astype(jnp.bfloat16)


def contract_second(state, wide):
    value = jnp.einsum("isbc,ijcd->jsbd", state, wide, preferred_element_type=jnp.float32)
    return value.astype(jnp.bfloat16)


def stepwise(stem_state, branch_mats, branch_modes, out_proj, groups):
    slabs = stem_state.shape[3]
    inner = stem_state.shape[4]
    state = stem_state.reshape(2, slabs, inner, inner)
    peers = lax.axis_size("modes")
    width_part = inner // peers
    for leg in range(branch_mats.shape[0]):

        def advance(branch, current):
            wide = widen(branch_mats[leg][branch])
            return lax.cond(
                branch_modes[leg][branch] == 0, contract_first, contract_second, current, wide
            )

        state = lax.fori_loop(0, branch_mats.shape[1], advance, state)
        pieces = state.reshape(2, slabs, inner, peers, width_part)
        pieces = jnp.transpose(pieces, (3, 0, 1, 2, 4)).reshape(peers, 2, slabs, inner * width_part)
        pieces = lax.all_to_all(pieces, "modes", split_axis=0, concat_axis=0, tiled=True)
        pieces = pieces.reshape(peers, 2, slabs, inner, width_part)
        state = jnp.transpose(pieces, (1, 2, 3, 0, 4)).reshape(2, slabs, inner, inner)
    stem_len = out_proj.shape[2]
    out_len = out_proj.shape[3]
    row_total = slabs * inner * inner // stem_len
    rows = state.reshape(2, row_total, stem_len)
    chosen = groups.reshape(row_total)
    piece = lax.all_gather(out_proj, "half", axis=0, tiled=True)
    wides = jax.vmap(widen)(piece)
    product = jnp.einsum("irk,gijkd->gjrd", rows, wides, preferred_element_type=jnp.float32)
    owners = jnp.arange(piece.shape[0], dtype=jnp.int32)
    keep = chosen[None, :] == owners[:, None]
    products = jnp.where(keep[:, None, :, None], product, 0.0)
    result = jnp.sum(products, axis=0).astype(jnp.bfloat16)
    return result.reshape(1, 1, 2, row_total, out_len)


def dot(left, right):
    return jnp.dot(left, right, preferred_element_type=jnp.float32)


def wide_of(top):
    inner = top.shape[0]
    real_part, imag_part = top[:, :inner], top[:, inner:]
    return jnp.concatenate([top, jnp.concatenate([-imag_part, real_part], axis=1)], axis=0)


def normal(top):
    largest = jnp.max(jnp.abs(top), axis=(0, 1), keepdims=True)
    largest = jnp.where(largest > 0.0, largest, 1.0)
    return top / largest, largest


def fused(
    sizes,
    state_ref,
    mats_hbm,
    modes_hbm,
    proj_ref,
    groups_hbm,
    out_ref,
    modes_ref,
    groups_ref,
    mats,
    got,
    leave,
    back,
    weights,
    local_sem,
    first_send,
    first_recv,
    last_send,
    last_recv,
    x_send,
    x_recv,
    y_send,
    y_recv,
    core_send,
    core_recv,
):
    peers, legs, branches, slabs, inner, depth = sizes
    width = inner // peers
    me = lax.axis_index("modes")
    row = lax.axis_index("slices")
    home = lax.axis_index("half")
    core = lax.rem(home, 2)
    sibling = home + 1 - 2 * core
    across = lax.rem(home + 2, 4)
    across_sibling = lax.rem(sibling + 2, 4)
    other_row = 1 - row
    part = got.shape[2]
    half_depth = depth // 2
    piece = half_depth // CHUNKS

    load_modes = pltpu.make_async_copy(modes_hbm, modes_ref, local_sem.at[3])
    load_modes.start()
    load_mats = pltpu.make_async_copy(mats_hbm, mats, local_sem.at[0])
    load_mats.start()
    load_own = pltpu.make_async_copy(
        state_ref.at[:, pl.ds(me * part, part), :], got.at[me], local_sem.at[1]
    )
    load_own.start()
    load_proj = pltpu.make_async_copy(proj_ref, weights.at[home], local_sem.at[2])
    load_proj.start()
    load_groups = pltpu.make_async_copy(groups_hbm, groups_ref, local_sem.at[4])
    load_groups.start()

    barrier = pltpu.get_barrier_semaphore()
    for step in range(1, peers):
        pl.semaphore_signal(
            barrier, inc=1, device_id={"modes": lax.rem(me + step, peers)}, device_id_type=MESH
        )
    pl.semaphore_signal(barrier, inc=1, device_id={"half": sibling}, device_id_type=MESH)
    pl.semaphore_signal(barrier, inc=1, device_id={"half": across}, device_id_type=MESH)
    pl.semaphore_signal(barrier, inc=1, device_id={"slices": other_row}, device_id_type=MESH)
    pl.semaphore_wait(barrier, peers + 2)

    first = []
    for step in range(1, peers):
        target = lax.rem(me + step, peers)
        copy = pltpu.make_async_remote_copy(
            src_ref=state_ref.at[:, pl.ds(target * part, part), :],
            dst_ref=got.at[me],
            send_sem=first_send.at[step - 1],
            recv_sem=first_recv.at[step - 1],
            device_id={"modes": target},
            device_id_type=MESH,
        )
        copy.start()
        first.append(copy)

    def rows_of(which, chunk):
        return pl.ds(which * half_depth + chunk * piece, piece)

    over_x, over_y, over_core = [], [], []
    for chunk in range(CHUNKS):
        copy = pltpu.make_async_remote_copy(
            src_ref=proj_ref.at[:, rows_of(row, chunk), :],
            dst_ref=weights.at[home, :, rows_of(row, chunk), :],
            send_sem=x_send.at[chunk],
            recv_sem=x_recv.at[chunk],
            device_id={"half": across},
            device_id_type=MESH,
        )
        copy.start()
        over_x.append(copy)
    own = pltpu.make_async_remote_copy(
        src_ref=proj_ref,
        dst_ref=weights.at[home],
        send_sem=core_send.at[0],
        recv_sem=core_recv.at[0],
        device_id={"half": sibling},
        device_id_type=MESH,
    )
    own.start()

    def to_core(which, chunk, number):
        copy = pltpu.make_async_remote_copy(
            src_ref=weights.at[across, :, rows_of(which, chunk), :],
            dst_ref=weights.at[across, :, rows_of(which, chunk), :],
            send_sem=core_send.at[number],
            recv_sem=core_recv.at[number],
            device_id={"half": sibling},
            device_id_type=MESH,
        )
        copy.start()
        over_core.append(copy)

    def hand_on(chunk):
        over_x[chunk].wait_recv()
        copy = pltpu.make_async_remote_copy(
            src_ref=weights.at[across, :, rows_of(row, chunk), :],
            dst_ref=weights.at[across, :, rows_of(row, chunk), :],
            send_sem=y_send.at[chunk],
            recv_sem=y_recv.at[chunk],
            device_id={"slices": other_row},
            device_id_type=MESH,
        )
        copy.start()
        over_y.append(copy)
        to_core(row, chunk, 1 + chunk)

    def take_in(chunk):
        over_y[chunk].wait_recv()
        to_core(other_row, chunk, 1 + CHUNKS + chunk)

    load_modes.wait()
    load_mats.wait()
    lanes = lax.broadcasted_iota(jnp.int32, (inner, 2 * inner), 1)
    sublanes = lax.broadcasted_iota(jnp.int32, (inner, 2 * inner), 0)
    identity = jnp.where(lanes == sublanes, 1.0, 0.0).astype(jnp.float32)
    over_b, over_c = [], []
    for leg in range(legs):
        top = jnp.concatenate([mats[leg, 0, 0], mats[leg, 0, 1]], axis=1).astype(jnp.float32)
        is_b = modes_ref[leg, 0] == 0
        over_b.append(jnp.where(is_b, top, identity))
        over_c.append(jnp.where(is_b, identity, top))
    for branch in range(1, branches):
        for leg in range(legs):
            is_b = modes_ref[leg, branch] == 0
            top = jnp.concatenate([mats[leg, branch, 0], mats[leg, branch, 1]], axis=1)
            chosen = jnp.where(is_b, over_b[leg], over_c[leg]).astype(jnp.bfloat16)
            value = dot(chosen, wide_of(top))
            over_b[leg] = jnp.where(is_b, value, over_b[leg])
            over_c[leg] = jnp.where(is_b, over_c[leg], value)
    hand_on(0)
    gains = []
    wides = []
    for leg in range(legs):
        scaled, gain = normal(over_c[leg])
        gains.append(gain)
        wides.append(wide_of(scaled.astype(jnp.bfloat16)))
        scaled, gain = normal(over_b[leg])
        gains.append(gain)
        over_b[leg] = scaled.astype(jnp.bfloat16)

    hand_on(1)
    load_own.wait()
    for copy in first:
        copy.wait()
    values = jnp.concatenate(
        [jnp.concatenate([got[m, 0], got[m, 1]], axis=1) for m in range(peers)], axis=0
    )
    block = lax.broadcasted_iota(jnp.int32, (part, inner), 1) // width
    for leg in range(legs):
        product = dot(values, wides[leg])
        swapped = []
        for m in range(peers):
            both = []
            for comp in range(2):
                taken = None
                for t in range(peers):
                    tile = product[t * part : (t + 1) * part, comp * inner : (comp + 1) * inner]
                    shift = (t - m) * width % inner
                    if shift:
                        tile = pltpu.roll(tile, shift, 1)
                    taken = tile if taken is None else jnp.where(block == t, tile, taken)
                both.append(taken)
            swapped.append(jnp.concatenate(both, axis=1))
        values = jnp.concatenate(swapped, axis=0).astype(jnp.bfloat16)
        if leg == 1:
            hand_on(2)
            take_in(0)
    for m in range(peers):
        leave[m] = values[m * part : (m + 1) * part]

    last = []
    for step in range(1, peers):
        target = lax.rem(me + step, peers)
        copy = pltpu.make_async_remote_copy(
            src_ref=leave.at[target],
            dst_ref=back.at[me],
            send_sem=last_send.at[step - 1],
            recv_sem=last_recv.at[step - 1],
            device_id={"modes": target},
            device_id_type=MESH,
        )
        copy.start()
        last.append(copy)
    back[me] = leave[me]
    hand_on(3)
    take_in(1)

    total = over_b[0]
    for leg in range(1, legs):
        total = dot(total, wide_of(over_b[leg])).astype(jnp.bfloat16)
    stacked = jnp.concatenate([total[:, :inner], total[:, inner:]], axis=0)
    quad = depth // inner
    short = inner // quad
    target_row = lax.broadcasted_iota(jnp.int32, (inner, inner), 0)
    source_col = lax.broadcasted_iota(jnp.int32, (inner, inner), 1)
    order = (source_col % quad) * short + source_col // quad == target_row
    order = jnp.where(order, 1.0, 0.0).astype(jnp.bfloat16)
    turned = lax.dot_general(
        order, stacked, (((1,), (1,)), ((), ())), preferred_element_type=jnp.float32
    ).astype(jnp.bfloat16)
    real_part, imag_part = turned[:, :inner], turned[:, inner:]
    left = jnp.concatenate(
        [
            jnp.concatenate([real_part, -imag_part], axis=1),
            jnp.concatenate([imag_part, real_part], axis=1),
        ],
        axis=0,
    )
    take_in(2)
    take_in(3)

    for copy in last:
        copy.wait()
    arrived = jnp.concatenate([back[m] for m in range(peers)], axis=0)
    right = jnp.concatenate(
        [
            jnp.concatenate(
                [
                    arrived[s * inner : (s + 1) * inner, comp * inner : (comp + 1) * inner]
                    for s in range(slabs)
                ],
                axis=1,
            )
            for comp in range(2)
        ],
        axis=0,
    )
    final = dot(left, right).astype(jnp.bfloat16)
    rows = jnp.concatenate(
        [
            jnp.concatenate(
                [
                    final[
                        comp * inner + q * short : comp * inner + (q + 1) * short,
                        s * inner : (s + 1) * inner,
                    ]
                    for q in range(quad)
                ],
                axis=1,
            )
            for comp in range(2)
            for s in range(slabs)
        ],
        axis=0,
    )
    count = slabs * short
    load_groups.wait()
    spread = jnp.broadcast_to(groups_ref[...].astype(jnp.float32), (count, count))
    on_diagonal = lax.broadcasted_iota(jnp.int32, (count, count), 0)
    on_diagonal = on_diagonal == lax.broadcasted_iota(jnp.int32, (count, count), 1)
    named = jnp.sum(jnp.where(on_diagonal, spread, 0.0), axis=1, keepdims=True)
    real_sum = jnp.zeros(out_ref.shape[1:], jnp.float32)
    imag_sum = jnp.zeros(out_ref.shape[1:], jnp.float32)

    def project(group, real_sum, imag_sum):
        by_real = dot(rows, weights[group, 0])
        by_imag = dot(rows, weights[group, 1])
        here = named == group.astype(jnp.float32)
        real_sum = jnp.where(here, by_real[:count] - by_imag[count:], real_sum)
        imag_sum = jnp.where(here, by_imag[:count] + by_real[count:], imag_sum)
        return real_sum, imag_sum

    load_proj.wait()
    real_sum, imag_sum = project(home, real_sum, imag_sum)
    own.wait()
    real_sum, imag_sum = project(sibling, real_sum, imag_sum)
    real_sum, imag_sum = project(across, real_sum, imag_sum)
    for copy in over_core:
        copy.wait()
    real_sum, imag_sum = project(across_sibling, real_sum, imag_sum)
    for gain in [jnp.minimum(g, 1.0) for g in gains] + [jnp.maximum(g, 1.0) for g in gains]:
        real_sum = real_sum * gain
        imag_sum = imag_sum * gain
    out_ref[0] = real_sum.astype(jnp.bfloat16)
    out_ref[1] = imag_sum.astype(jnp.bfloat16)
    for copy in over_x:
        copy.wait_send()
    for copy in over_y:
        copy.wait_send()


def local(stem_state, branch_mats, branch_modes, out_proj, groups):
    slabs, inner = stem_state.shape[3], stem_state.shape[4]
    legs, branches = branch_mats.shape[:2]
    depth, out_len = out_proj.shape[2:]
    peers = lax.axis_size("modes")
    rows = slabs * inner
    row_total = rows * inner // depth
    part = rows // peers
    bf16 = jnp.bfloat16
    whole = pl.BlockSpec(memory_space=pl.ANY)
    result = pl.pallas_call(
        functools.partial(fused, (peers, legs, branches, slabs, inner, depth)),
        out_shape=jax.ShapeDtypeStruct((2, row_total, out_len), bf16),
        in_specs=[
            whole,
            whole,
            whole,
            whole,
            whole,
        ],
        out_specs=pl.BlockSpec(memory_space=pltpu.VMEM),
        scratch_shapes=[
            pltpu.SMEM(branch_modes.shape, jnp.int32),
            pltpu.VMEM((1, row_total), jnp.int32),
            pltpu.VMEM(branch_mats.shape, bf16),
            pltpu.VMEM((peers, 2, part, inner), bf16),
            pltpu.VMEM((peers, part, 2 * inner), bf16),
            pltpu.VMEM((peers, part, 2 * inner), bf16),
            pltpu.VMEM((lax.axis_size("half"), 2, depth, out_len), bf16),
            pltpu.SemaphoreType.DMA((5,)),
            pltpu.SemaphoreType.DMA((peers - 1,)),
            pltpu.SemaphoreType.DMA((peers - 1,)),
            pltpu.SemaphoreType.DMA((peers - 1,)),
            pltpu.SemaphoreType.DMA((peers - 1,)),
            pltpu.SemaphoreType.DMA((CHUNKS,)),
            pltpu.SemaphoreType.DMA((CHUNKS,)),
            pltpu.SemaphoreType.DMA((CHUNKS,)),
            pltpu.SemaphoreType.DMA((CHUNKS,)),
            pltpu.SemaphoreType.DMA((1 + 2 * CHUNKS,)),
            pltpu.SemaphoreType.DMA((1 + 2 * CHUNKS,)),
        ],
        compiler_params=pltpu.CompilerParams(
            collective_id=0, has_side_effects=True, vmem_limit_bytes=60 * 1024 * 1024
        ),
    )(
        stem_state.reshape(2, rows, inner),
        branch_mats,
        branch_modes,
        out_proj.reshape(out_proj.shape[1:]),
        groups.reshape(1, row_total),
    )
    return result.reshape(1, 1, 2, row_total, out_len)


def solution(mesh):
    placed = (
        P(None, ("slices", "modes"), "half", None, None, None),
        P(),
        P(),
        P("half", None, None, None),
        P(("slices", "modes"), "half", None, None),
    )
    sizes = dict(mesh.shape)
    in_kernel = sizes["half"] == 4 and sizes["slices"] == 2 and sizes["modes"] <= 4
    return jax.shard_map(
        local if in_kernel else stepwise,
        mesh=mesh,
        in_specs=placed,
        out_specs=P(("slices", "modes"), "half", None, None, None),
        check_vma=False,
    )
```

```python
import functools

import jax
import jax.numpy as jnp
from jax import lax
from jax.experimental import pallas as pl
from jax.experimental.pallas import tpu as pltpu
from jax.sharding import PartitionSpec as P

MESH = pl.DeviceIdType.MESH
CHUNKS = 4


def widen(matrix):
    real_part = matrix[0]
    imag_part = matrix[1]
    return jnp.stack([jnp.stack([real_part, imag_part]), jnp.stack([-imag_part, real_part])])


def contract_first(state, wide):
    value = jnp.einsum("isbc,ijbd->jsdc", state, wide, preferred_element_type=jnp.float32)
    return value.astype(jnp.bfloat16)


def contract_second(state, wide):
    value = jnp.einsum("isbc,ijcd->jsbd", state, wide, preferred_element_type=jnp.float32)
    return value.astype(jnp.bfloat16)


def stepwise(stem_state, branch_mats, branch_modes, out_proj, groups):
    slabs = stem_state.shape[3]
    inner = stem_state.shape[4]
    state = stem_state.reshape(2, slabs, inner, inner)
    peers = lax.axis_size("modes")
    width_part = inner // peers
    for leg in range(branch_mats.shape[0]):

        def advance(branch, current):
            wide = widen(branch_mats[leg][branch])
            return lax.cond(
                branch_modes[leg][branch] == 0, contract_first, contract_second, current, wide
            )

        state = lax.fori_loop(0, branch_mats.shape[1], advance, state)
        pieces = state.reshape(2, slabs, inner, peers, width_part)
        pieces = jnp.transpose(pieces, (3, 0, 1, 2, 4)).reshape(peers, 2, slabs, inner * width_part)
        pieces = lax.all_to_all(pieces, "modes", split_axis=0, concat_axis=0, tiled=True)
        pieces = pieces.reshape(peers, 2, slabs, inner, width_part)
        state = jnp.transpose(pieces, (1, 2, 3, 0, 4)).reshape(2, slabs, inner, inner)
    stem_len = out_proj.shape[2]
    out_len = out_proj.shape[3]
    row_total = slabs * inner * inner // stem_len
    rows = state.reshape(2, row_total, stem_len)
    chosen = groups.reshape(row_total)
    piece = lax.all_gather(out_proj, "half", axis=0, tiled=True)
    wides = jax.vmap(widen)(piece)
    product = jnp.einsum("irk,gijkd->gjrd", rows, wides, preferred_element_type=jnp.float32)
    owners = jnp.arange(piece.shape[0], dtype=jnp.int32)
    keep = chosen[None, :] == owners[:, None]
    products = jnp.where(keep[:, None, :, None], product, 0.0)
    result = jnp.sum(products, axis=0).astype(jnp.bfloat16)
    return result.reshape(1, 1, 2, row_total, out_len)


def dot(left, right):
    return jnp.dot(left, right, preferred_element_type=jnp.float32)


def wide_of(top):
    inner = top.shape[0]
    real_part, imag_part = top[:, :inner], top[:, inner:]
    return jnp.concatenate([top, jnp.concatenate([-imag_part, real_part], axis=1)], axis=0)


def normal(top):
    largest = jnp.max(jnp.abs(top), axis=(0, 1), keepdims=True)
    largest = jnp.where(largest > 0.0, largest, 1.0)
    return top * (1.0 / largest), largest


def fused(
    sizes,
    state_ref,
    mats_hbm,
    modes_hbm,
    proj_ref,
    groups_hbm,
    out_ref,
    modes_ref,
    groups_ref,
    mats,
    past,
    got,
    leave,
    back,
    weights,
    local_sem,
    first_send,
    first_recv,
    last_send,
    last_recv,
    x_send,
    x_recv,
    y_send,
    y_recv,
    core_send,
    core_recv,
):
    peers, legs, branches, slabs, inner, depth = sizes
    width = inner // peers
    me = lax.axis_index("modes")
    row = lax.axis_index("slices")
    home = lax.axis_index("half")
    core = lax.rem(home, 2)
    sibling = home + 1 - 2 * core
    across = lax.rem(home + 2, 4)
    across_sibling = lax.rem(sibling + 2, 4)
    other_row = 1 - row
    part = got.shape[2]
    half_depth = depth // 2
    piece = half_depth // CHUNKS

    load_modes = pltpu.make_async_copy(modes_hbm, modes_ref, local_sem.at[3])
    load_modes.start()
    load_mats = pltpu.make_async_copy(mats_hbm, mats, local_sem.at[0])
    load_mats.start()
    load_own = pltpu.make_async_copy(
        state_ref.at[:, pl.ds(me * part, part), :], got.at[me], local_sem.at[1]
    )
    load_own.start()
    load_proj = pltpu.make_async_copy(proj_ref, weights.at[home], local_sem.at[2])
    load_proj.start()
    load_groups = pltpu.make_async_copy(groups_hbm, groups_ref, local_sem.at[4])
    load_groups.start()

    barrier = pltpu.get_barrier_semaphore()
    for step in range(1, peers):
        pl.semaphore_signal(
            barrier, inc=1, device_id={"modes": lax.rem(me + step, peers)}, device_id_type=MESH
        )
    pl.semaphore_signal(barrier, inc=1, device_id={"half": sibling}, device_id_type=MESH)
    pl.semaphore_signal(barrier, inc=1, device_id={"half": across}, device_id_type=MESH)
    pl.semaphore_signal(barrier, inc=1, device_id={"slices": other_row}, device_id_type=MESH)
    pl.semaphore_wait(barrier, peers + 2)

    first = []
    for step in range(1, peers):
        target = lax.rem(me + step, peers)
        copy = pltpu.make_async_remote_copy(
            src_ref=state_ref.at[:, pl.ds(target * part, part), :],
            dst_ref=got.at[me],
            send_sem=first_send.at[step - 1],
            recv_sem=first_recv.at[step - 1],
            device_id={"modes": target},
            device_id_type=MESH,
        )
        copy.start()
        first.append(copy)

    def rows_of(which, chunk):
        return pl.ds(which * half_depth + chunk * piece, piece)

    over_x, over_y, over_core = [], [], []
    for chunk in range(CHUNKS):
        copy = pltpu.make_async_remote_copy(
            src_ref=proj_ref.at[:, rows_of(row, chunk), :],
            dst_ref=weights.at[home, :, rows_of(row, chunk), :],
            send_sem=x_send.at[chunk],
            recv_sem=x_recv.at[chunk],
            device_id={"half": across},
            device_id_type=MESH,
        )
        copy.start()
        over_x.append(copy)
    own = pltpu.make_async_remote_copy(
        src_ref=proj_ref,
        dst_ref=weights.at[home],
        send_sem=core_send.at[0],
        recv_sem=core_recv.at[0],
        device_id={"half": sibling},
        device_id_type=MESH,
    )
    own.start()

    def to_core(which, chunk, number):
        copy = pltpu.make_async_remote_copy(
            src_ref=weights.at[across, :, rows_of(which, chunk), :],
            dst_ref=weights.at[across, :, rows_of(which, chunk), :],
            send_sem=core_send.at[number],
            recv_sem=core_recv.at[number],
            device_id={"half": sibling},
            device_id_type=MESH,
        )
        copy.start()
        over_core.append(copy)

    def hand_on(chunk):
        over_x[chunk].wait_recv()
        copy = pltpu.make_async_remote_copy(
            src_ref=weights.at[across, :, rows_of(row, chunk), :],
            dst_ref=weights.at[across, :, rows_of(row, chunk), :],
            send_sem=y_send.at[chunk],
            recv_sem=y_recv.at[chunk],
            device_id={"slices": other_row},
            device_id_type=MESH,
        )
        copy.start()
        over_y.append(copy)
        to_core(row, chunk, 1 + chunk)

    def take_in(chunk):
        over_y[chunk].wait_recv()
        to_core(other_row, chunk, 1 + CHUNKS + chunk)

    load_modes.wait()
    load_mats.wait()
    lanes = lax.broadcasted_iota(jnp.int32, (inner, 2 * inner), 1)
    sublanes = lax.broadcasted_iota(jnp.int32, (inner, 2 * inner), 0)
    identity = jnp.where(lanes == sublanes, 1.0, 0.0).astype(jnp.bfloat16)
    last_b, last_c = {}, {}

    def start_leg(leg):
        past[leg, 0] = identity
        past[leg, 1, :, :inner] = mats[leg, 0, 0]
        past[leg, 1, :, inner:] = mats[leg, 0, 1]
        is_b = modes_ref[leg, 0] == 0
        last_b[leg] = jnp.where(is_b, 1, 0)
        last_c[leg] = jnp.where(is_b, 0, 1)

    def next_branch(leg, branch):
        is_b = modes_ref[leg, branch] == 0
        top = jnp.concatenate([mats[leg, branch, 0], mats[leg, branch, 1]], axis=1)
        before = past[leg, jnp.where(is_b, last_b[leg], last_c[leg])]
        past[leg, branch + 1] = dot(before, wide_of(top)).astype(jnp.bfloat16)
        last_b[leg] = jnp.where(is_b, branch + 1, last_b[leg])
        last_c[leg] = jnp.where(is_b, last_c[leg], branch + 1)

    block = lax.broadcasted_iota(jnp.int32, (part, inner), 1) // width

    def apply_leg(values, wide):
        product = dot(values, wide)
        swapped = []
        for m in range(peers):
            both = []
            for comp in range(2):
                taken = None
                for t in range(peers):
                    tile = product[t * part : (t + 1) * part, comp * inner : (comp + 1) * inner]
                    shift = (t - m) * width % inner
                    if shift:
                        tile = pltpu.roll(tile, shift, 1)
                    taken = tile if taken is None else jnp.where(block == t, tile, taken)
                both.append(taken)
            swapped.append(jnp.concatenate(both, axis=1))
        return jnp.concatenate(swapped, axis=0).astype(jnp.bfloat16)

    gains = []

    def scaled(top):
        top, gain = normal(top.astype(jnp.float32))
        gains.append(gain)
        return top.astype(jnp.bfloat16)

    early = min(2, legs)
    for leg in range(early):
        start_leg(leg)
    for branch in range(1, branches):
        for leg in range(early):
            next_branch(leg, branch)
    load_own.wait()
    for copy in first:
        copy.wait()
    hand_on(0)
    values = jnp.concatenate(
        [jnp.concatenate([got[m, 0], got[m, 1]], axis=1) for m in range(peers)], axis=0
    )
    for leg in range(early):
        values = apply_leg(values, wide_of(past[leg, last_c[leg]]))
    for leg in range(early, legs):
        start_leg(leg)
    for branch in range(1, branches):
        for leg in range(early, legs):
            next_branch(leg, branch)
    hand_on(1)
    hand_on(2)
    for leg in range(early, legs):
        values = apply_leg(values, wide_of(scaled(past[leg, last_c[leg]])))
    for m in range(peers):
        leave[m] = values[m * part : (m + 1) * part]

    last = []
    for step in range(1, peers):
        target = lax.rem(me + step, peers)
        copy = pltpu.make_async_remote_copy(
            src_ref=leave.at[target],
            dst_ref=back.at[me],
            send_sem=last_send.at[step - 1],
            recv_sem=last_recv.at[step - 1],
            device_id={"modes": target},
            device_id_type=MESH,
        )
        copy.start()
        last.append(copy)
    back[me] = leave[me]
    hand_on(3)
    take_in(0)

    factors = [past[leg, last_b[leg]] for leg in range(legs)]
    while len(factors) > 1:
        pairs = [
            scaled(dot(factors[i], wide_of(factors[i + 1]))) for i in range(0, len(factors) - 1, 2)
        ]
        factors = pairs + factors[len(pairs) * 2 :]
    total = factors[0]
    stacked = jnp.concatenate([total[:, :inner], total[:, inner:]], axis=0)
    quad = depth // inner
    short = inner // quad
    target_row = lax.broadcasted_iota(jnp.int32, (inner, inner), 0)
    source_col = lax.broadcasted_iota(jnp.int32, (inner, inner), 1)
    order = (source_col % quad) * short + source_col // quad == target_row
    order = jnp.where(order, 1.0, 0.0).astype(jnp.bfloat16)
    turned = lax.dot_general(
        order, stacked, (((1,), (1,)), ((), ())), preferred_element_type=jnp.float32
    ).astype(jnp.bfloat16)
    real_part, imag_part = turned[:, :inner], turned[:, inner:]
    left = jnp.concatenate(
        [
            jnp.concatenate([real_part, -imag_part], axis=1),
            jnp.concatenate([imag_part, real_part], axis=1),
        ],
        axis=0,
    )
    take_in(1)
    take_in(2)
    take_in(3)

    for copy in last:
        copy.wait()
    arrived = jnp.concatenate([back[m] for m in range(peers)], axis=0)
    right = jnp.concatenate(
        [
            jnp.concatenate(
                [
                    arrived[s * inner : (s + 1) * inner, comp * inner : (comp + 1) * inner]
                    for s in range(slabs)
                ],
                axis=1,
            )
            for comp in range(2)
        ],
        axis=0,
    )
    final = dot(left, right).astype(jnp.bfloat16)
    rows = jnp.concatenate(
        [
            jnp.concatenate(
                [
                    final[
                        comp * inner + q * short : comp * inner + (q + 1) * short,
                        s * inner : (s + 1) * inner,
                    ]
                    for q in range(quad)
                ],
                axis=1,
            )
            for comp in range(2)
            for s in range(slabs)
        ],
        axis=0,
    )
    count = slabs * short
    load_groups.wait()
    spread = jnp.broadcast_to(groups_ref[...].astype(jnp.float32), (count, count))
    on_diagonal = lax.broadcasted_iota(jnp.int32, (count, count), 0)
    on_diagonal = on_diagonal == lax.broadcasted_iota(jnp.int32, (count, count), 1)
    named = jnp.sum(jnp.where(on_diagonal, spread, 0.0), axis=1, keepdims=True)
    real_sum = jnp.zeros(out_ref.shape[1:], jnp.float32)
    imag_sum = jnp.zeros(out_ref.shape[1:], jnp.float32)

    def project(group, real_sum, imag_sum):
        by_real = dot(rows, weights[group, 0])
        by_imag = dot(rows, weights[group, 1])
        here = named == group.astype(jnp.float32)
        real_sum = jnp.where(here, by_real[:count] - by_imag[count:], real_sum)
        imag_sum = jnp.where(here, by_imag[:count] + by_real[count:], imag_sum)
        return real_sum, imag_sum

    load_proj.wait()
    real_sum, imag_sum = project(home, real_sum, imag_sum)
    own.wait()
    real_sum, imag_sum = project(sibling, real_sum, imag_sum)
    real_sum, imag_sum = project(across, real_sum, imag_sum)
    for copy in over_core:
        copy.wait()
    real_sum, imag_sum = project(across_sibling, real_sum, imag_sum)
    for gain in [jnp.minimum(g, 1.0) for g in gains] + [jnp.maximum(g, 1.0) for g in gains]:
        real_sum = real_sum * gain
        imag_sum = imag_sum * gain
    out_ref[0] = real_sum
    out_ref[1] = imag_sum
    for copy in over_x:
        copy.wait_send()
    for copy in over_y:
        copy.wait_send()


def local(stem_state, branch_mats, branch_modes, out_proj, groups):
    slabs, inner = stem_state.shape[3], stem_state.shape[4]
    legs, branches = branch_mats.shape[:2]
    depth, out_len = out_proj.shape[2:]
    peers = lax.axis_size("modes")
    rows = slabs * inner
    row_total = rows * inner // depth
    part = rows // peers
    bf16 = jnp.bfloat16
    whole = pl.BlockSpec(memory_space=pl.ANY)
    result = pl.pallas_call(
        functools.partial(fused, (peers, legs, branches, slabs, inner, depth)),
        out_shape=jax.ShapeDtypeStruct((2, row_total, out_len), jnp.float32),
        in_specs=[
            whole,
            whole,
            whole,
            whole,
            whole,
        ],
        out_specs=pl.BlockSpec(memory_space=pltpu.VMEM),
        scratch_shapes=[
            pltpu.SMEM(branch_modes.shape, jnp.int32),
            pltpu.VMEM((1, row_total), jnp.int32),
            pltpu.VMEM(branch_mats.shape, bf16),
            pltpu.VMEM((legs, branches + 1, inner, 2 * inner), bf16),
            pltpu.VMEM((peers, 2, part, inner), bf16),
            pltpu.VMEM((peers, part, 2 * inner), bf16),
            pltpu.VMEM((peers, part, 2 * inner), bf16),
            pltpu.VMEM((lax.axis_size("half"), 2, depth, out_len), bf16),
            pltpu.SemaphoreType.DMA((5,)),
            pltpu.SemaphoreType.DMA((peers - 1,)),
            pltpu.SemaphoreType.DMA((peers - 1,)),
            pltpu.SemaphoreType.DMA((peers - 1,)),
            pltpu.SemaphoreType.DMA((peers - 1,)),
            pltpu.SemaphoreType.DMA((CHUNKS,)),
            pltpu.SemaphoreType.DMA((CHUNKS,)),
            pltpu.SemaphoreType.DMA((CHUNKS,)),
            pltpu.SemaphoreType.DMA((CHUNKS,)),
            pltpu.SemaphoreType.DMA((1 + 2 * CHUNKS,)),
            pltpu.SemaphoreType.DMA((1 + 2 * CHUNKS,)),
        ],
        compiler_params=pltpu.CompilerParams(
            collective_id=0, has_side_effects=True, vmem_limit_bytes=60 * 1024 * 1024
        ),
    )(
        stem_state.reshape(2, rows, inner),
        branch_mats,
        branch_modes,
        out_proj.reshape(out_proj.shape[1:]),
        groups.reshape(1, row_total),
    )
    return result.astype(bf16).reshape(1, 1, 2, row_total, out_len)


def solution(mesh):
    placed = (
        P(None, ("slices", "modes"), "half", None, None, None),
        P(),
        P(),
        P("half", None, None, None),
        P(("slices", "modes"), "half", None, None),
    )
    sizes = dict(mesh.shape)
    in_kernel = sizes["half"] == 4 and sizes["slices"] == 2 and sizes["modes"] <= 4
    return jax.shard_map(
        local if in_kernel else stepwise,
        mesh=mesh,
        in_specs=placed,
        out_specs=P(("slices", "modes"), "half", None, None, None),
        check_vma=False,
    )
```

```python
import functools

import jax
import jax.numpy as jnp
from jax import lax
from jax.experimental import pallas as pl
from jax.experimental.pallas import tpu as pltpu
from jax.sharding import PartitionSpec as P

MESH = pl.DeviceIdType.MESH
CHUNKS = 8
DIRECT = 5


def widen(matrix):
    real_part = matrix[0]
    imag_part = matrix[1]
    return jnp.stack([jnp.stack([real_part, imag_part]), jnp.stack([-imag_part, real_part])])


def contract_first(state, wide):
    value = jnp.einsum("isbc,ijbd->jsdc", state, wide, preferred_element_type=jnp.float32)
    return value.astype(jnp.bfloat16)


def contract_second(state, wide):
    value = jnp.einsum("isbc,ijcd->jsbd", state, wide, preferred_element_type=jnp.float32)
    return value.astype(jnp.bfloat16)


def stepwise(stem_state, branch_mats, branch_modes, out_proj, groups):
    slabs = stem_state.shape[3]
    inner = stem_state.shape[4]
    state = stem_state.reshape(2, slabs, inner, inner)
    peers = lax.axis_size("modes")
    width_part = inner // peers
    for leg in range(branch_mats.shape[0]):

        def advance(branch, current):
            wide = widen(branch_mats[leg][branch])
            return lax.cond(
                branch_modes[leg][branch] == 0, contract_first, contract_second, current, wide
            )

        state = lax.fori_loop(0, branch_mats.shape[1], advance, state)
        pieces = state.reshape(2, slabs, inner, peers, width_part)
        pieces = jnp.transpose(pieces, (3, 0, 1, 2, 4)).reshape(peers, 2, slabs, inner * width_part)
        pieces = lax.all_to_all(pieces, "modes", split_axis=0, concat_axis=0, tiled=True)
        pieces = pieces.reshape(peers, 2, slabs, inner, width_part)
        state = jnp.transpose(pieces, (1, 2, 3, 0, 4)).reshape(2, slabs, inner, inner)
    stem_len = out_proj.shape[2]
    out_len = out_proj.shape[3]
    row_total = slabs * inner * inner // stem_len
    rows = state.reshape(2, row_total, stem_len)
    chosen = groups.reshape(row_total)
    piece = lax.all_gather(out_proj, "half", axis=0, tiled=True)
    wides = jax.vmap(widen)(piece)
    product = jnp.einsum("irk,gijkd->gjrd", rows, wides, preferred_element_type=jnp.float32)
    owners = jnp.arange(piece.shape[0], dtype=jnp.int32)
    keep = chosen[None, :] == owners[:, None]
    products = jnp.where(keep[:, None, :, None], product, 0.0)
    result = jnp.sum(products, axis=0).astype(jnp.bfloat16)
    return result.reshape(1, 1, 2, row_total, out_len)


def dot(left, right):
    return jnp.dot(left, right, preferred_element_type=jnp.float32)


def wide_of(top):
    inner = top.shape[0]
    real_part, imag_part = top[:, :inner], top[:, inner:]
    return jnp.concatenate([top, jnp.concatenate([-imag_part, real_part], axis=1)], axis=0)


def normal(top):
    largest = jnp.max(jnp.abs(top), axis=(0, 1), keepdims=True)
    largest = jnp.where(largest > 0.0, largest, 1.0)
    return top * (1.0 / largest), largest


def fused(
    sizes,
    state_ref,
    mats_hbm,
    modes_hbm,
    proj_ref,
    groups_hbm,
    out_ref,
    modes_ref,
    groups_ref,
    mats,
    past,
    got,
    leave,
    back,
    weights,
    local_sem,
    first_send,
    first_recv,
    last_send,
    last_recv,
    x_send,
    x_recv,
    y_send,
    y_recv,
    core_send,
    core_recv,
):
    peers, legs, branches, slabs, inner, depth = sizes
    width = inner // peers
    me = lax.axis_index("modes")
    row = lax.axis_index("slices")
    home = lax.axis_index("half")
    core = lax.rem(home, 2)
    sibling = home + 1 - 2 * core
    across = lax.rem(home + 2, 4)
    across_sibling = lax.rem(sibling + 2, 4)
    other_row = 1 - row
    part = got.shape[2]
    piece = depth // CHUNKS
    handed = CHUNKS - DIRECT

    barrier = pltpu.get_barrier_semaphore()
    for step in range(1, peers):
        pl.semaphore_signal(
            barrier, inc=1, device_id={"modes": lax.rem(me + step, peers)}, device_id_type=MESH
        )
    pl.semaphore_signal(barrier, inc=1, device_id={"half": sibling}, device_id_type=MESH)
    pl.semaphore_signal(barrier, inc=1, device_id={"half": across}, device_id_type=MESH)
    pl.semaphore_signal(barrier, inc=1, device_id={"slices": other_row}, device_id_type=MESH)

    load_modes = pltpu.make_async_copy(modes_hbm, modes_ref, local_sem.at[0])
    load_modes.start()
    load_mats = []
    for leg in range(legs):
        load_mats.append(
            pltpu.make_async_copy(mats_hbm.at[leg], mats.at[leg], local_sem.at[4 + leg])
        )
        load_mats[leg].start()
    load_own = pltpu.make_async_copy(
        state_ref.at[:, pl.ds(me * part, part), :], got.at[me], local_sem.at[1]
    )
    load_own.start()
    pl.semaphore_wait(barrier, peers + 2)

    first = []
    for step in range(1, peers):
        target = lax.rem(me + step, peers)
        copy = pltpu.make_async_remote_copy(
            src_ref=state_ref.at[:, pl.ds(target * part, part), :],
            dst_ref=got.at[me],
            send_sem=first_send.at[step - 1],
            recv_sem=first_recv.at[step - 1],
            device_id={"modes": target},
            device_id_type=MESH,
        )
        copy.start()
        first.append(copy)

    def rows_of(which, chunk):
        forward = pl.multiple_of(which * (CHUNKS - 1) * piece + (1 - 2 * which) * chunk * piece, piece)
        return pl.ds(forward, piece)

    over_x, over_y, over_core = [], [], []
    for chunk in range(DIRECT):
        copy = pltpu.make_async_remote_copy(
            src_ref=proj_ref.at[:, rows_of(row, chunk), :],
            dst_ref=weights.at[home, :, rows_of(row, chunk), :],
            send_sem=x_send.at[chunk],
            recv_sem=x_recv.at[chunk],
            device_id={"half": across},
            device_id_type=MESH,
        )
        copy.start()
        over_x.append(copy)
    own = pltpu.make_async_remote_copy(
        src_ref=proj_ref,
        dst_ref=weights.at[home],
        send_sem=core_send.at[0],
        recv_sem=core_recv.at[0],
        device_id={"half": sibling},
        device_id_type=MESH,
    )
    load_proj = pltpu.make_async_copy(proj_ref, weights.at[home], local_sem.at[2])
    load_groups = pltpu.make_async_copy(groups_hbm, groups_ref, local_sem.at[3])

    def to_core(which, chunk, number):
        copy = pltpu.make_async_remote_copy(
            src_ref=weights.at[across, :, rows_of(which, chunk), :],
            dst_ref=weights.at[across, :, rows_of(which, chunk), :],
            send_sem=core_send.at[number],
            recv_sem=core_recv.at[number],
            device_id={"half": sibling},
            device_id_type=MESH,
        )
        copy.start()
        over_core.append(copy)

    def from_x(chunk):
        over_x[chunk].wait_recv()
        if chunk < handed:
            copy = pltpu.make_async_remote_copy(
                src_ref=weights.at[across, :, rows_of(row, chunk), :],
                dst_ref=weights.at[across, :, rows_of(row, chunk), :],
                send_sem=y_send.at[chunk],
                recv_sem=y_recv.at[chunk],
                device_id={"slices": other_row},
                device_id_type=MESH,
            )
            copy.start()
            over_y.append(copy)
        to_core(row, chunk, 1 + chunk)

    def from_y(chunk):
        over_y[chunk].wait_recv()
        to_core(other_row, chunk, 1 + DIRECT + chunk)

    load_modes.wait()
    lanes = lax.broadcasted_iota(jnp.int32, (inner, 2 * inner), 1)
    sublanes = lax.broadcasted_iota(jnp.int32, (inner, 2 * inner), 0)
    identity = jnp.where(lanes == sublanes, 1.0, 0.0).astype(jnp.bfloat16)
    last_b, last_c = {}, {}

    def start_leg(leg):
        load_mats[leg].wait()
        past[leg, 0] = identity
        past[leg, 1, :, :inner] = mats[leg, 0, 0]
        past[leg, 1, :, inner:] = mats[leg, 0, 1]
        is_b = modes_ref[leg, 0] == 0
        last_b[leg] = jnp.where(is_b, 1, 0)
        last_c[leg] = jnp.where(is_b, 0, 1)

    def next_branch(leg, branch):
        is_b = modes_ref[leg, branch] == 0
        top = jnp.concatenate([mats[leg, branch, 0], mats[leg, branch, 1]], axis=1)
        before = past[leg, jnp.where(is_b, last_b[leg], last_c[leg])]
        past[leg, branch + 1] = dot(before, wide_of(top)).astype(jnp.bfloat16)
        last_b[leg] = jnp.where(is_b, branch + 1, last_b[leg])
        last_c[leg] = jnp.where(is_b, last_c[leg], branch + 1)

    block = lax.broadcasted_iota(jnp.int32, (part, inner), 1) // width

    def apply_leg(values, wide):
        product = dot(values, wide)
        swapped = []
        for m in range(peers):
            both = []
            for comp in range(2):
                taken = None
                for t in range(peers):
                    tile = product[t * part : (t + 1) * part, comp * inner : (comp + 1) * inner]
                    shift = (t - m) * width % inner
                    if shift:
                        tile = pltpu.roll(tile, shift, 1)
                    taken = tile if taken is None else jnp.where(block == t, tile, taken)
                both.append(taken)
            swapped.append(jnp.concatenate(both, axis=1))
        return jnp.concatenate(swapped, axis=0).astype(jnp.bfloat16)

    gains = []

    def scaled(top):
        top, gain = normal(top.astype(jnp.float32))
        gains.append(gain)
        return top.astype(jnp.bfloat16)

    early = min(2, legs)
    for group in (range(early), range(early, legs)):
        for leg in group:
            start_leg(leg)
        for branch in range(1, branches):
            for leg in group:
                next_branch(leg, branch)
        if group[0] == 0:
            own.start()
            load_proj.start()
            load_groups.start()
    wides = []
    for leg in range(legs):
        top = past[leg, last_c[leg]]
        wides.append(wide_of(top if leg < early else scaled(top)))
    from_x(0)
    load_own.wait()
    for copy in first:
        copy.wait()
    values = jnp.concatenate(
        [jnp.concatenate([got[m, 0], got[m, 1]], axis=1) for m in range(peers)], axis=0
    )
    values = apply_leg(values, wides[0])
    from_x(1)
    for leg in range(1, legs - 1):
        values = apply_leg(values, wides[leg])
    from_x(2)
    values = apply_leg(values, wides[legs - 1])
    for m in range(peers):
        leave[m] = values[m * part : (m + 1) * part]

    last = []
    for step in range(1, peers):
        target = lax.rem(me + step, peers)
        copy = pltpu.make_async_remote_copy(
            src_ref=leave.at[target],
            dst_ref=back.at[me],
            send_sem=last_send.at[step - 1],
            recv_sem=last_recv.at[step - 1],
            device_id={"modes": target},
            device_id_type=MESH,
        )
        copy.start()
        last.append(copy)
    back[me] = leave[me]

    factors = [past[leg, last_b[leg]] for leg in range(legs)]
    while len(factors) > 1:
        pairs = [
            scaled(dot(factors[i], wide_of(factors[i + 1]))) for i in range(0, len(factors) - 1, 2)
        ]
        factors = pairs + factors[len(pairs) * 2 :]
    total = factors[0]
    stacked = jnp.concatenate([total[:, :inner], total[:, inner:]], axis=0)
    quad = depth // inner
    short = inner // quad
    target_row = lax.broadcasted_iota(jnp.int32, (inner, inner), 0)
    source_col = lax.broadcasted_iota(jnp.int32, (inner, inner), 1)
    order = (source_col % quad) * short + source_col // quad == target_row
    order = jnp.where(order, 1.0, 0.0).astype(jnp.bfloat16)
    turned = lax.dot_general(
        order, stacked, (((1,), (1,)), ((), ())), preferred_element_type=jnp.float32
    ).astype(jnp.bfloat16)
    real_part, imag_part = turned[:, :inner], turned[:, inner:]
    left = jnp.concatenate(
        [
            jnp.concatenate([real_part, -imag_part], axis=1),
            jnp.concatenate([imag_part, real_part], axis=1),
        ],
        axis=0,
    )
    from_y(0)
    from_x(3)
    from_y(1)
    from_x(4)
    from_y(2)

    for copy in last:
        copy.wait()
    arrived = jnp.concatenate([back[m] for m in range(peers)], axis=0)
    right = jnp.concatenate(
        [
            jnp.concatenate(
                [
                    arrived[s * inner : (s + 1) * inner, comp * inner : (comp + 1) * inner]
                    for s in range(slabs)
                ],
                axis=1,
            )
            for comp in range(2)
        ],
        axis=0,
    )
    final = dot(left, right).astype(jnp.bfloat16)
    rows = jnp.concatenate(
        [
            jnp.concatenate(
                [
                    final[
                        comp * inner + q * short : comp * inner + (q + 1) * short,
                        s * inner : (s + 1) * inner,
                    ]
                    for q in range(quad)
                ],
                axis=1,
            )
            for comp in range(2)
            for s in range(slabs)
        ],
        axis=0,
    )
    count = slabs * short
    load_groups.wait()
    spread = jnp.broadcast_to(groups_ref[...].astype(jnp.float32), (count, count))
    on_diagonal = lax.broadcasted_iota(jnp.int32, (count, count), 0)
    on_diagonal = on_diagonal == lax.broadcasted_iota(jnp.int32, (count, count), 1)
    named = jnp.sum(jnp.where(on_diagonal, spread, 0.0), axis=1, keepdims=True)
    real_sum = jnp.zeros(out_ref.shape[1:], jnp.float32)
    imag_sum = jnp.zeros(out_ref.shape[1:], jnp.float32)

    def project(group, real_sum, imag_sum):
        by_real = dot(rows, weights[group, 0])
        by_imag = dot(rows, weights[group, 1])
        here = named == group.astype(jnp.float32)
        real_sum = jnp.where(here, by_real[:count] - by_imag[count:], real_sum)
        imag_sum = jnp.where(here, by_imag[:count] + by_real[count:], imag_sum)
        return real_sum, imag_sum

    load_proj.wait()
    real_sum, imag_sum = project(home, real_sum, imag_sum)
    own.wait()
    real_sum, imag_sum = project(sibling, real_sum, imag_sum)
    real_sum, imag_sum = project(across, real_sum, imag_sum)
    for copy in over_core:
        copy.wait()
    real_sum, imag_sum = project(across_sibling, real_sum, imag_sum)
    for gain in [jnp.minimum(g, 1.0) for g in gains] + [jnp.maximum(g, 1.0) for g in gains]:
        real_sum = real_sum * gain
        imag_sum = imag_sum * gain
    out_ref[0] = real_sum
    out_ref[1] = imag_sum
    for copy in over_x:
        copy.wait_send()
    for copy in over_y:
        copy.wait_send()


def local(stem_state, branch_mats, branch_modes, out_proj, groups):
    slabs, inner = stem_state.shape[3], stem_state.shape[4]
    legs, branches = branch_mats.shape[:2]
    depth, out_len = out_proj.shape[2:]
    peers = lax.axis_size("modes")
    rows = slabs * inner
    row_total = rows * inner // depth
    part = rows // peers
    bf16 = jnp.bfloat16
    whole = pl.BlockSpec(memory_space=pl.ANY)
    result = pl.pallas_call(
        functools.partial(fused, (peers, legs, branches, slabs, inner, depth)),
        out_shape=jax.ShapeDtypeStruct((2, row_total, out_len), jnp.float32),
        in_specs=[
            whole,
            whole,
            whole,
            whole,
            whole,
        ],
        out_specs=pl.BlockSpec(memory_space=pltpu.VMEM),
        scratch_shapes=[
            pltpu.SMEM(branch_modes.shape, jnp.int32),
            pltpu.VMEM((1, row_total), jnp.int32),
            pltpu.VMEM(branch_mats.shape, bf16),
            pltpu.VMEM((legs, branches + 1, inner, 2 * inner), bf16),
            pltpu.VMEM((peers, 2, part, inner), bf16),
            pltpu.VMEM((peers, part, 2 * inner), bf16),
            pltpu.VMEM((peers, part, 2 * inner), bf16),
            pltpu.VMEM((lax.axis_size("half"), 2, depth, out_len), bf16),
            pltpu.SemaphoreType.DMA((4 + legs,)),
            pltpu.SemaphoreType.DMA((peers - 1,)),
            pltpu.SemaphoreType.DMA((peers - 1,)),
            pltpu.SemaphoreType.DMA((peers - 1,)),
            pltpu.SemaphoreType.DMA((peers - 1,)),
            pltpu.SemaphoreType.DMA((DIRECT,)),
            pltpu.SemaphoreType.DMA((DIRECT,)),
            pltpu.SemaphoreType.DMA((CHUNKS - DIRECT,)),
            pltpu.SemaphoreType.DMA((CHUNKS - DIRECT,)),
            pltpu.SemaphoreType.DMA((1 + CHUNKS,)),
            pltpu.SemaphoreType.DMA((1 + CHUNKS,)),
        ],
        compiler_params=pltpu.CompilerParams(
            collective_id=0, has_side_effects=True, vmem_limit_bytes=60 * 1024 * 1024
        ),
    )(
        stem_state.reshape(2, rows, inner),
        branch_mats,
        branch_modes,
        out_proj.reshape(out_proj.shape[1:]),
        groups.reshape(1, row_total),
    )
    return result.astype(bf16).reshape(1, 1, 2, row_total, out_len)


def solution(mesh):
    placed = (
        P(None, ("slices", "modes"), "half", None, None, None),
        P(),
        P(),
        P("half", None, None, None),
        P(("slices", "modes"), "half", None, None),
    )
    sizes = dict(mesh.shape)
    in_kernel = sizes["half"] == 4 and sizes["slices"] == 2 and sizes["modes"] <= 4
    return jax.shard_map(
        local if in_kernel else stepwise,
        mesh=mesh,
        in_specs=placed,
        out_specs=P(("slices", "modes"), "half", None, None, None),
        check_vma=False,
    )
```

```python
import functools

import jax
import jax.numpy as jnp
from jax import lax
from jax.experimental import pallas as pl
from jax.experimental.pallas import tpu as pltpu
from jax.sharding import PartitionSpec as P

MESH = pl.DeviceIdType.MESH
CHUNKS = 8
DIRECT = 5
WAVES = 2


def widen(matrix):
    real_part = matrix[0]
    imag_part = matrix[1]
    return jnp.stack([jnp.stack([real_part, imag_part]), jnp.stack([-imag_part, real_part])])


def contract_first(state, wide):
    value = jnp.einsum("isbc,ijbd->jsdc", state, wide, preferred_element_type=jnp.float32)
    return value.astype(jnp.bfloat16)


def contract_second(state, wide):
    value = jnp.einsum("isbc,ijcd->jsbd", state, wide, preferred_element_type=jnp.float32)
    return value.astype(jnp.bfloat16)


def stepwise(stem_state, branch_mats, branch_modes, out_proj, groups):
    slabs = stem_state.shape[3]
    inner = stem_state.shape[4]
    state = stem_state.reshape(2, slabs, inner, inner)
    peers = lax.axis_size("modes")
    width_part = inner // peers
    for leg in range(branch_mats.shape[0]):

        def advance(branch, current):
            wide = widen(branch_mats[leg][branch])
            return lax.cond(
                branch_modes[leg][branch] == 0, contract_first, contract_second, current, wide
            )

        state = lax.fori_loop(0, branch_mats.shape[1], advance, state)
        pieces = state.reshape(2, slabs, inner, peers, width_part)
        pieces = jnp.transpose(pieces, (3, 0, 1, 2, 4)).reshape(peers, 2, slabs, inner * width_part)
        pieces = lax.all_to_all(pieces, "modes", split_axis=0, concat_axis=0, tiled=True)
        pieces = pieces.reshape(peers, 2, slabs, inner, width_part)
        state = jnp.transpose(pieces, (1, 2, 3, 0, 4)).reshape(2, slabs, inner, inner)
    stem_len = out_proj.shape[2]
    out_len = out_proj.shape[3]
    row_total = slabs * inner * inner // stem_len
    rows = state.reshape(2, row_total, stem_len)
    chosen = groups.reshape(row_total)
    piece = lax.all_gather(out_proj, "half", axis=0, tiled=True)
    wides = jax.vmap(widen)(piece)
    product = jnp.einsum("irk,gijkd->gjrd", rows, wides, preferred_element_type=jnp.float32)
    owners = jnp.arange(piece.shape[0], dtype=jnp.int32)
    keep = chosen[None, :] == owners[:, None]
    products = jnp.where(keep[:, None, :, None], product, 0.0)
    result = jnp.sum(products, axis=0).astype(jnp.bfloat16)
    return result.reshape(1, 1, 2, row_total, out_len)


def dot(left, right):
    return jnp.dot(left, right, preferred_element_type=jnp.float32)


def wide_of(top):
    inner = top.shape[0]
    real_part, imag_part = top[:, :inner], top[:, inner:]
    return jnp.concatenate([top, jnp.concatenate([-imag_part, real_part], axis=1)], axis=0)


def normal(top):
    largest = jnp.max(jnp.abs(top), axis=(0, 1), keepdims=True)
    largest = jnp.where(largest > 0.0, largest, 1.0)
    return top * (1.0 / largest), largest


def fused(
    sizes,
    state_ref,
    mats_hbm,
    modes_hbm,
    proj_ref,
    groups_hbm,
    out_ref,
    modes_ref,
    groups_ref,
    mats,
    past,
    got,
    leave,
    back,
    weights,
    local_sem,
    first_send,
    first_recv,
    last_send,
    last_recv,
    x_send,
    x_recv,
    y_send,
    y_recv,
    core_send,
    core_recv,
):
    peers, legs, branches, slabs, inner, depth = sizes
    width = inner // peers
    me = lax.axis_index("modes")
    row = lax.axis_index("slices")
    home = lax.axis_index("half")
    core = lax.rem(home, 2)
    sibling = home + 1 - 2 * core
    across = lax.rem(home + 2, 4)
    across_sibling = lax.rem(sibling + 2, 4)
    other_row = 1 - row
    part = got.shape[2]
    piece = depth // CHUNKS
    handed = CHUNKS - DIRECT

    barrier = pltpu.get_barrier_semaphore()
    for step in range(1, peers):
        pl.semaphore_signal(
            barrier, inc=1, device_id={"modes": lax.rem(me + step, peers)}, device_id_type=MESH
        )
    pl.semaphore_signal(barrier, inc=1, device_id={"half": sibling}, device_id_type=MESH)
    pl.semaphore_signal(barrier, inc=1, device_id={"half": across}, device_id_type=MESH)
    pl.semaphore_signal(barrier, inc=1, device_id={"slices": other_row}, device_id_type=MESH)

    load_modes = pltpu.make_async_copy(modes_hbm, modes_ref, local_sem.at[0])
    load_modes.start()
    load_mats = []
    for leg in range(legs):
        load_mats.append(
            pltpu.make_async_copy(mats_hbm.at[leg], mats.at[leg], local_sem.at[4 + leg])
        )
        load_mats[leg].start()
    load_own = pltpu.make_async_copy(
        state_ref.at[:, pl.ds(me * part, part), :], got.at[me], local_sem.at[1]
    )
    load_own.start()
    pl.semaphore_wait(barrier, peers + 2)

    stripe = part // WAVES
    first = []
    for wave in range(WAVES):
        for step in range(1, peers):
            target = lax.rem(me + step, peers)
            copy = pltpu.make_async_remote_copy(
                src_ref=state_ref.at[:, pl.ds(target * part + wave * stripe, stripe), :],
                dst_ref=got.at[me, :, pl.ds(wave * stripe, stripe), :],
                send_sem=first_send.at[wave, step - 1],
                recv_sem=first_recv.at[wave, step - 1],
                device_id={"modes": target},
                device_id_type=MESH,
            )
            copy.start()
            first.append(copy)

    def rows_of(which, chunk):
        forward = pl.multiple_of(which * (CHUNKS - 1) * piece + (1 - 2 * which) * chunk * piece, piece)
        return pl.ds(forward, piece)

    over_x, over_y, over_core = [], [], []
    for chunk in range(DIRECT):
        copy = pltpu.make_async_remote_copy(
            src_ref=proj_ref.at[:, rows_of(row, chunk), :],
            dst_ref=weights.at[home, :, rows_of(row, chunk), :],
            send_sem=x_send.at[chunk],
            recv_sem=x_recv.at[chunk],
            device_id={"half": across},
            device_id_type=MESH,
        )
        copy.start()
        over_x.append(copy)
    own = pltpu.make_async_remote_copy(
        src_ref=proj_ref,
        dst_ref=weights.at[home],
        send_sem=core_send.at[0],
        recv_sem=core_recv.at[0],
        device_id={"half": sibling},
        device_id_type=MESH,
    )
    load_proj = pltpu.make_async_copy(proj_ref, weights.at[home], local_sem.at[2])
    load_groups = pltpu.make_async_copy(groups_hbm, groups_ref, local_sem.at[3])

    def to_core(which, chunk, number):
        copy = pltpu.make_async_remote_copy(
            src_ref=weights.at[across, :, rows_of(which, chunk), :],
            dst_ref=weights.at[across, :, rows_of(which, chunk), :],
            send_sem=core_send.at[number],
            recv_sem=core_recv.at[number],
            device_id={"half": sibling},
            device_id_type=MESH,
        )
        copy.start()
        over_core.append(copy)

    def from_x(chunk):
        over_x[chunk].wait_recv()
        if chunk < handed:
            copy = pltpu.make_async_remote_copy(
                src_ref=weights.at[across, :, rows_of(row, chunk), :],
                dst_ref=weights.at[across, :, rows_of(row, chunk), :],
                send_sem=y_send.at[chunk],
                recv_sem=y_recv.at[chunk],
                device_id={"slices": other_row},
                device_id_type=MESH,
            )
            copy.start()
            over_y.append(copy)
        to_core(row, chunk, 1 + chunk)

    def from_y(chunk):
        over_y[chunk].wait_recv()
        to_core(other_row, chunk, 1 + DIRECT + chunk)

    load_modes.wait()
    lanes = lax.broadcasted_iota(jnp.int32, (inner, 2 * inner), 1)
    sublanes = lax.broadcasted_iota(jnp.int32, (inner, 2 * inner), 0)
    identity = jnp.where(lanes == sublanes, 1.0, 0.0).astype(jnp.bfloat16)
    last_b, last_c = {}, {}

    def start_leg(leg):
        load_mats[leg].wait()
        past[leg, 0] = identity
        past[leg, 1, :, :inner] = mats[leg, 0, 0]
        past[leg, 1, :, inner:] = mats[leg, 0, 1]
        is_b = modes_ref[leg, 0] == 0
        last_b[leg] = jnp.where(is_b, 1, 0)
        last_c[leg] = jnp.where(is_b, 0, 1)

    def next_branch(leg, branch):
        is_b = modes_ref[leg, branch] == 0
        top = jnp.concatenate([mats[leg, branch, 0], mats[leg, branch, 1]], axis=1)
        before = past[leg, jnp.where(is_b, last_b[leg], last_c[leg])]
        past[leg, branch + 1] = dot(before, wide_of(top)).astype(jnp.bfloat16)
        last_b[leg] = jnp.where(is_b, branch + 1, last_b[leg])
        last_c[leg] = jnp.where(is_b, last_c[leg], branch + 1)

    block = lax.broadcasted_iota(jnp.int32, (stripe, inner), 1) // width

    def apply_leg(values, wide):
        product = dot(values, wide)
        swapped = []
        for m in range(peers):
            both = []
            for comp in range(2):
                taken = None
                for t in range(peers):
                    tile = product[t * stripe : (t + 1) * stripe, comp * inner : (comp + 1) * inner]
                    shift = (t - m) * width % inner
                    if shift:
                        tile = pltpu.roll(tile, shift, 1)
                    taken = tile if taken is None else jnp.where(block == t, tile, taken)
                both.append(taken)
            swapped.append(jnp.concatenate(both, axis=1))
        return jnp.concatenate(swapped, axis=0).astype(jnp.bfloat16)

    gains = []

    def scaled(top):
        top, gain = normal(top.astype(jnp.float32))
        gains.append(gain)
        return top.astype(jnp.bfloat16)

    early = min(2, legs)
    for group in (range(early), range(early, legs)):
        for leg in group:
            start_leg(leg)
        for branch in range(1, branches):
            for leg in group:
                next_branch(leg, branch)
        if group[0] == 0:
            own.start()
            load_proj.start()
            load_groups.start()
    wides = []
    for leg in range(legs):
        top = past[leg, last_c[leg]]
        wides.append(wide_of(top if leg < early else scaled(top)))
    load_own.wait()
    last = []
    for wave in range(WAVES):
        strip = pl.ds(wave * stripe, stripe)
        for copy in first[wave * (peers - 1) : (wave + 1) * (peers - 1)]:
            copy.wait()
        from_x(wave)
        values = jnp.concatenate(
            [
                jnp.concatenate([got[m, 0, strip, :], got[m, 1, strip, :]], axis=1)
                for m in range(peers)
            ],
            axis=0,
        )
        for leg in range(legs):
            values = apply_leg(values, wides[leg])
        for m in range(peers):
            leave[m, strip, :] = values[m * stripe : (m + 1) * stripe]
        for step in range(1, peers):
            target = lax.rem(me + step, peers)
            copy = pltpu.make_async_remote_copy(
                src_ref=leave.at[target, strip, :],
                dst_ref=back.at[me, strip, :],
                send_sem=last_send.at[wave, step - 1],
                recv_sem=last_recv.at[wave, step - 1],
                device_id={"modes": target},
                device_id_type=MESH,
            )
            copy.start()
            last.append(copy)
    back[me] = leave[me]

    factors = [past[leg, last_b[leg]] for leg in range(legs)]
    while len(factors) > 1:
        pairs = [
            scaled(dot(factors[i], wide_of(factors[i + 1]))) for i in range(0, len(factors) - 1, 2)
        ]
        factors = pairs + factors[len(pairs) * 2 :]
    total = factors[0]
    stacked = jnp.concatenate([total[:, :inner], total[:, inner:]], axis=0)
    quad = depth // inner
    short = inner // quad
    target_row = lax.broadcasted_iota(jnp.int32, (inner, inner), 0)
    source_col = lax.broadcasted_iota(jnp.int32, (inner, inner), 1)
    order = (source_col % quad) * short + source_col // quad == target_row
    order = jnp.where(order, 1.0, 0.0).astype(jnp.bfloat16)
    turned = lax.dot_general(
        order, stacked, (((1,), (1,)), ((), ())), preferred_element_type=jnp.float32
    ).astype(jnp.bfloat16)
    real_part, imag_part = turned[:, :inner], turned[:, inner:]
    left = jnp.concatenate(
        [
            jnp.concatenate([real_part, -imag_part], axis=1),
            jnp.concatenate([imag_part, real_part], axis=1),
        ],
        axis=0,
    )
    for chunk in range(WAVES, DIRECT - 1):
        from_x(chunk)
        from_y(chunk - WAVES)

    for copy in last:
        copy.wait()
    arrived = jnp.concatenate([back[m] for m in range(peers)], axis=0)
    right = jnp.concatenate(
        [
            jnp.concatenate(
                [
                    arrived[s * inner : (s + 1) * inner, comp * inner : (comp + 1) * inner]
                    for s in range(slabs)
                ],
                axis=1,
            )
            for comp in range(2)
        ],
        axis=0,
    )
    final = dot(left, right).astype(jnp.bfloat16)
    rows = jnp.concatenate(
        [
            jnp.concatenate(
                [
                    final[
                        comp * inner + q * short : comp * inner + (q + 1) * short,
                        s * inner : (s + 1) * inner,
                    ]
                    for q in range(quad)
                ],
                axis=1,
            )
            for comp in range(2)
            for s in range(slabs)
        ],
        axis=0,
    )
    count = slabs * short
    load_groups.wait()
    spread = jnp.broadcast_to(groups_ref[...].astype(jnp.float32), (count, count))
    on_diagonal = lax.broadcasted_iota(jnp.int32, (count, count), 0)
    on_diagonal = on_diagonal == lax.broadcasted_iota(jnp.int32, (count, count), 1)
    named = jnp.sum(jnp.where(on_diagonal, spread, 0.0), axis=1, keepdims=True)
    real_sum = jnp.zeros(out_ref.shape[1:], jnp.float32)
    imag_sum = jnp.zeros(out_ref.shape[1:], jnp.float32)

    def project(group, real_sum, imag_sum):
        by_real = dot(rows, weights[group, 0])
        by_imag = dot(rows, weights[group, 1])
        here = named == group.astype(jnp.float32)
        real_sum = jnp.where(here, by_real[:count] - by_imag[count:], real_sum)
        imag_sum = jnp.where(here, by_imag[:count] + by_real[count:], imag_sum)
        return real_sum, imag_sum

    load_proj.wait()
    real_sum, imag_sum = project(home, real_sum, imag_sum)
    own.wait()
    real_sum, imag_sum = project(sibling, real_sum, imag_sum)
    from_x(DIRECT - 1)
    for chunk in range(DIRECT - 1 - WAVES, handed):
        from_y(chunk)
    real_sum, imag_sum = project(across, real_sum, imag_sum)
    for copy in over_core:
        copy.wait()
    real_sum, imag_sum = project(across_sibling, real_sum, imag_sum)
    for gain in [jnp.minimum(g, 1.0) for g in gains] + [jnp.maximum(g, 1.0) for g in gains]:
        real_sum = real_sum * gain
        imag_sum = imag_sum * gain
    out_ref[0] = real_sum.astype(jnp.bfloat16)
    out_ref[1] = imag_sum.astype(jnp.bfloat16)
    for copy in over_x:
        copy.wait_send()
    for copy in over_y:
        copy.wait_send()


def local(stem_state, branch_mats, branch_modes, out_proj, groups):
    slabs, inner = stem_state.shape[3], stem_state.shape[4]
    legs, branches = branch_mats.shape[:2]
    depth, out_len = out_proj.shape[2:]
    peers = lax.axis_size("modes")
    rows = slabs * inner
    row_total = rows * inner // depth
    part = rows // peers
    bf16 = jnp.bfloat16
    whole = pl.BlockSpec(memory_space=pl.ANY)
    result = pl.pallas_call(
        functools.partial(fused, (peers, legs, branches, slabs, inner, depth)),
        out_shape=jax.ShapeDtypeStruct((2, row_total, out_len), bf16),
        in_specs=[
            whole,
            whole,
            whole,
            whole,
            whole,
        ],
        out_specs=pl.BlockSpec(memory_space=pltpu.VMEM),
        scratch_shapes=[
            pltpu.SMEM(branch_modes.shape, jnp.int32),
            pltpu.VMEM((1, row_total), jnp.int32),
            pltpu.VMEM(branch_mats.shape, bf16),
            pltpu.VMEM((legs, branches + 1, inner, 2 * inner), bf16),
            pltpu.VMEM((peers, 2, part, inner), bf16),
            pltpu.VMEM((peers, part, 2 * inner), bf16),
            pltpu.VMEM((peers, part, 2 * inner), bf16),
            pltpu.VMEM((lax.axis_size("half"), 2, depth, out_len), bf16),
            pltpu.SemaphoreType.DMA((4 + legs,)),
            pltpu.SemaphoreType.DMA((WAVES, peers - 1)),
            pltpu.SemaphoreType.DMA((WAVES, peers - 1)),
            pltpu.SemaphoreType.DMA((WAVES, peers - 1)),
            pltpu.SemaphoreType.DMA((WAVES, peers - 1)),
            pltpu.SemaphoreType.DMA((DIRECT,)),
            pltpu.SemaphoreType.DMA((DIRECT,)),
            pltpu.SemaphoreType.DMA((CHUNKS - DIRECT,)),
            pltpu.SemaphoreType.DMA((CHUNKS - DIRECT,)),
            pltpu.SemaphoreType.DMA((1 + CHUNKS,)),
            pltpu.SemaphoreType.DMA((1 + CHUNKS,)),
        ],
        compiler_params=pltpu.CompilerParams(
            collective_id=0, has_side_effects=True, vmem_limit_bytes=60 * 1024 * 1024
        ),
    )(
        stem_state.reshape(2, rows, inner),
        branch_mats,
        branch_modes,
        out_proj.reshape(out_proj.shape[1:]),
        groups.reshape(1, row_total),
    )
    return result.reshape(1, 1, 2, row_total, out_len)


def solution(mesh):
    placed = (
        P(None, ("slices", "modes"), "half", None, None, None),
        P(),
        P(),
        P("half", None, None, None),
        P(("slices", "modes"), "half", None, None),
    )
    sizes = dict(mesh.shape)
    in_kernel = sizes["half"] == 4 and sizes["slices"] == 2 and sizes["modes"] <= 4
    return jax.shard_map(
        local if in_kernel else stepwise,
        mesh=mesh,
        in_specs=placed,
        out_specs=P(("slices", "modes"), "half", None, None, None),
        check_vma=False,
    )
```

```python
import functools

import jax
import jax.numpy as jnp
from jax import lax
from jax.experimental import pallas as pl
from jax.experimental.pallas import tpu as pltpu
from jax.sharding import PartitionSpec as P

MESH = pl.DeviceIdType.MESH
CHUNKS = 16
DIRECT = 9
WAVES = 2


def widen(matrix):
    real_part = matrix[0]
    imag_part = matrix[1]
    return jnp.stack([jnp.stack([real_part, imag_part]), jnp.stack([-imag_part, real_part])])


def contract_first(state, wide):
    value = jnp.einsum("isbc,ijbd->jsdc", state, wide, preferred_element_type=jnp.float32)
    return value.astype(jnp.bfloat16)


def contract_second(state, wide):
    value = jnp.einsum("isbc,ijcd->jsbd", state, wide, preferred_element_type=jnp.float32)
    return value.astype(jnp.bfloat16)


def stepwise(stem_state, branch_mats, branch_modes, out_proj, groups):
    slabs = stem_state.shape[3]
    inner = stem_state.shape[4]
    state = stem_state.reshape(2, slabs, inner, inner)
    peers = lax.axis_size("modes")
    width_part = inner // peers
    for leg in range(branch_mats.shape[0]):

        def advance(branch, current):
            wide = widen(branch_mats[leg][branch])
            return lax.cond(
                branch_modes[leg][branch] == 0, contract_first, contract_second, current, wide
            )

        state = lax.fori_loop(0, branch_mats.shape[1], advance, state)
        pieces = state.reshape(2, slabs, inner, peers, width_part)
        pieces = jnp.transpose(pieces, (3, 0, 1, 2, 4)).reshape(peers, 2, slabs, inner * width_part)
        pieces = lax.all_to_all(pieces, "modes", split_axis=0, concat_axis=0, tiled=True)
        pieces = pieces.reshape(peers, 2, slabs, inner, width_part)
        state = jnp.transpose(pieces, (1, 2, 3, 0, 4)).reshape(2, slabs, inner, inner)
    stem_len = out_proj.shape[2]
    out_len = out_proj.shape[3]
    row_total = slabs * inner * inner // stem_len
    rows = state.reshape(2, row_total, stem_len)
    chosen = groups.reshape(row_total)
    piece = lax.all_gather(out_proj, "half", axis=0, tiled=True)
    wides = jax.vmap(widen)(piece)
    product = jnp.einsum("irk,gijkd->gjrd", rows, wides, preferred_element_type=jnp.float32)
    owners = jnp.arange(piece.shape[0], dtype=jnp.int32)
    keep = chosen[None, :] == owners[:, None]
    products = jnp.where(keep[:, None, :, None], product, 0.0)
    result = jnp.sum(products, axis=0).astype(jnp.bfloat16)
    return result.reshape(1, 1, 2, row_total, out_len)


def dot(left, right):
    return jnp.dot(left, right, preferred_element_type=jnp.float32)


def wide_of(top):
    inner = top.shape[0]
    real_part, imag_part = top[:, :inner], top[:, inner:]
    return jnp.concatenate([top, jnp.concatenate([-imag_part, real_part], axis=1)], axis=0)


def normal(top):
    largest = jnp.max(jnp.abs(top), axis=(0, 1), keepdims=True)
    largest = jnp.where(largest > 0.0, largest, 1.0)
    return top * (1.0 / largest), largest


def fused(
    sizes,
    state_ref,
    mats_hbm,
    modes_hbm,
    proj_ref,
    groups_hbm,
    out_ref,
    modes_ref,
    groups_ref,
    mats,
    past,
    got,
    leave,
    back,
    weights,
    local_sem,
    first_send,
    first_recv,
    last_send,
    last_recv,
    x_send,
    x_recv,
    y_send,
    y_recv,
    core_send,
    core_recv,
):
    peers, legs, branches, slabs, inner, depth = sizes
    width = inner // peers
    me = lax.axis_index("modes")
    row = lax.axis_index("slices")
    home = lax.axis_index("half")
    core = lax.rem(home, 2)
    sibling = home + 1 - 2 * core
    across = lax.rem(home + 2, 4)
    across_sibling = lax.rem(sibling + 2, 4)
    other_row = 1 - row
    part = got.shape[2]
    piece = depth // CHUNKS
    handed = CHUNKS - DIRECT

    barrier = pltpu.get_barrier_semaphore()
    for step in range(1, peers):
        pl.semaphore_signal(
            barrier, inc=1, device_id={"modes": lax.rem(me + step, peers)}, device_id_type=MESH
        )
    pl.semaphore_signal(barrier, inc=1, device_id={"half": sibling}, device_id_type=MESH)
    pl.semaphore_signal(barrier, inc=1, device_id={"half": across}, device_id_type=MESH)
    pl.semaphore_signal(barrier, inc=1, device_id={"slices": other_row}, device_id_type=MESH)

    load_modes = pltpu.make_async_copy(modes_hbm, modes_ref, local_sem.at[0])
    load_modes.start()
    load_mats = []
    for leg in range(legs):
        load_mats.append(
            pltpu.make_async_copy(mats_hbm.at[leg], mats.at[leg], local_sem.at[4 + leg])
        )
        load_mats[leg].start()
    load_own = pltpu.make_async_copy(
        state_ref.at[:, pl.ds(me * part, part), :], got.at[me], local_sem.at[1]
    )
    load_own.start()
    pl.semaphore_wait(barrier, peers + 2)

    stripe = part // WAVES
    first = []
    for wave in range(WAVES):
        for step in range(1, peers):
            target = lax.rem(me + step, peers)
            copy = pltpu.make_async_remote_copy(
                src_ref=state_ref.at[:, pl.ds(target * part + wave * stripe, stripe), :],
                dst_ref=got.at[me, :, pl.ds(wave * stripe, stripe), :],
                send_sem=first_send.at[wave, step - 1],
                recv_sem=first_recv.at[wave, step - 1],
                device_id={"modes": target},
                device_id_type=MESH,
            )
            copy.start()
            first.append(copy)

    def rows_of(which, chunk):
        forward = pl.multiple_of(which * (CHUNKS - 1) * piece + (1 - 2 * which) * chunk * piece, piece)
        return pl.ds(forward, piece)

    over_x, over_y, over_core = [], [], []
    for chunk in range(DIRECT):
        copy = pltpu.make_async_remote_copy(
            src_ref=proj_ref.at[:, rows_of(row, chunk), :],
            dst_ref=weights.at[home, :, rows_of(row, chunk), :],
            send_sem=x_send.at[chunk],
            recv_sem=x_recv.at[chunk],
            device_id={"half": across},
            device_id_type=MESH,
        )
        copy.start()
        over_x.append(copy)
    own = pltpu.make_async_remote_copy(
        src_ref=proj_ref,
        dst_ref=weights.at[home],
        send_sem=core_send.at[0],
        recv_sem=core_recv.at[0],
        device_id={"half": sibling},
        device_id_type=MESH,
    )
    load_proj = pltpu.make_async_copy(proj_ref, weights.at[home], local_sem.at[2])
    load_groups = pltpu.make_async_copy(groups_hbm, groups_ref, local_sem.at[3])

    def to_core(which, chunk, number):
        copy = pltpu.make_async_remote_copy(
            src_ref=weights.at[across, :, rows_of(which, chunk), :],
            dst_ref=weights.at[across, :, rows_of(which, chunk), :],
            send_sem=core_send.at[number],
            recv_sem=core_recv.at[number],
            device_id={"half": sibling},
            device_id_type=MESH,
        )
        copy.start()
        over_core.append(copy)

    def from_x(chunk):
        over_x[chunk].wait_recv()
        if chunk < handed:
            copy = pltpu.make_async_remote_copy(
                src_ref=weights.at[across, :, rows_of(row, chunk), :],
                dst_ref=weights.at[across, :, rows_of(row, chunk), :],
                send_sem=y_send.at[chunk],
                recv_sem=y_recv.at[chunk],
                device_id={"slices": other_row},
                device_id_type=MESH,
            )
            copy.start()
            over_y.append(copy)
        to_core(row, chunk, 1 + chunk)

    def from_y(chunk):
        over_y[chunk].wait_recv()
        to_core(other_row, chunk, 1 + DIRECT + chunk)

    load_modes.wait()
    lanes = lax.broadcasted_iota(jnp.int32, (inner, 2 * inner), 1)
    sublanes = lax.broadcasted_iota(jnp.int32, (inner, 2 * inner), 0)
    identity = jnp.where(lanes == sublanes, 1.0, 0.0).astype(jnp.bfloat16)
    last_b, last_c = {}, {}

    def start_leg(leg):
        load_mats[leg].wait()
        past[leg, 0] = identity
        past[leg, 1, :, :inner] = mats[leg, 0, 0]
        past[leg, 1, :, inner:] = mats[leg, 0, 1]
        is_b = modes_ref[leg, 0] == 0
        last_b[leg] = jnp.where(is_b, 1, 0)
        last_c[leg] = jnp.where(is_b, 0, 1)

    def next_branch(leg, branch):
        is_b = modes_ref[leg, branch] == 0
        top = jnp.concatenate([mats[leg, branch, 0], mats[leg, branch, 1]], axis=1)
        before = past[leg, jnp.where(is_b, last_b[leg], last_c[leg])]
        past[leg, branch + 1] = dot(before, wide_of(top)).astype(jnp.bfloat16)
        last_b[leg] = jnp.where(is_b, branch + 1, last_b[leg])
        last_c[leg] = jnp.where(is_b, last_c[leg], branch + 1)

    block = lax.broadcasted_iota(jnp.int32, (stripe, inner), 1) // width

    def apply_leg(values, wide):
        product = dot(values, wide)
        swapped = []
        for m in range(peers):
            both = []
            for comp in range(2):
                taken = None
                for t in range(peers):
                    tile = product[t * stripe : (t + 1) * stripe, comp * inner : (comp + 1) * inner]
                    shift = (t - m) * width % inner
                    if shift:
                        tile = pltpu.roll(tile, shift, 1)
                    taken = tile if taken is None else jnp.where(block == t, tile, taken)
                both.append(taken)
            swapped.append(jnp.concatenate(both, axis=1))
        return jnp.concatenate(swapped, axis=0).astype(jnp.bfloat16)

    gains = []

    def scaled(top):
        top, gain = normal(top.astype(jnp.float32))
        gains.append(gain)
        return top.astype(jnp.bfloat16)

    early = min(2, legs)
    for group in (range(early), range(early, legs)):
        for leg in group:
            start_leg(leg)
        for branch in range(1, branches):
            for leg in group:
                next_branch(leg, branch)
        if group[0] == 0:
            from_x(0)
            own.start()
            load_proj.start()
            load_groups.start()
    wides = []
    for leg in range(legs):
        top = past[leg, last_c[leg]]
        wides.append(wide_of(top if leg < early else scaled(top)))
    from_x(1)
    load_own.wait()
    last = []
    for wave in range(WAVES):
        strip = pl.ds(wave * stripe, stripe)
        for copy in first[wave * (peers - 1) : (wave + 1) * (peers - 1)]:
            copy.wait()
        values = jnp.concatenate(
            [
                jnp.concatenate([got[m, 0, strip, :], got[m, 1, strip, :]], axis=1)
                for m in range(peers)
            ],
            axis=0,
        )
        for leg in range(legs):
            values = apply_leg(values, wides[leg])
            if leg == legs // 2 - 1:
                from_x(2 + 2 * wave)
                if wave:
                    from_y(1)
        for m in range(peers):
            leave[m, strip, :] = values[m * stripe : (m + 1) * stripe]
        for step in range(1, peers):
            target = lax.rem(me + step, peers)
            copy = pltpu.make_async_remote_copy(
                src_ref=leave.at[target, strip, :],
                dst_ref=back.at[me, strip, :],
                send_sem=last_send.at[wave, step - 1],
                recv_sem=last_recv.at[wave, step - 1],
                device_id={"modes": target},
                device_id_type=MESH,
            )
            copy.start()
            last.append(copy)
        from_x(3 + 2 * wave)
        from_y(2 * wave)
    back[me] = leave[me]

    factors = [past[leg, last_b[leg]] for leg in range(legs)]
    while len(factors) > 1:
        pairs = [
            scaled(dot(factors[i], wide_of(factors[i + 1]))) for i in range(0, len(factors) - 1, 2)
        ]
        factors = pairs + factors[len(pairs) * 2 :]
    total = factors[0]
    stacked = jnp.concatenate([total[:, :inner], total[:, inner:]], axis=0)
    quad = depth // inner
    short = inner // quad
    target_row = lax.broadcasted_iota(jnp.int32, (inner, inner), 0)
    source_col = lax.broadcasted_iota(jnp.int32, (inner, inner), 1)
    order = (source_col % quad) * short + source_col // quad == target_row
    order = jnp.where(order, 1.0, 0.0).astype(jnp.bfloat16)
    turned = lax.dot_general(
        order, stacked, (((1,), (1,)), ((), ())), preferred_element_type=jnp.float32
    ).astype(jnp.bfloat16)
    real_part, imag_part = turned[:, :inner], turned[:, inner:]
    left = jnp.concatenate(
        [
            jnp.concatenate([real_part, -imag_part], axis=1),
            jnp.concatenate([imag_part, real_part], axis=1),
        ],
        axis=0,
    )
    from_x(6)
    from_y(3)
    from_y(4)
    from_x(7)
    from_y(5)
    for copy in last:
        copy.wait()
    arrived = jnp.concatenate([back[m] for m in range(peers)], axis=0)
    right = jnp.concatenate(
        [
            jnp.concatenate(
                [
                    arrived[s * inner : (s + 1) * inner, comp * inner : (comp + 1) * inner]
                    for s in range(slabs)
                ],
                axis=1,
            )
            for comp in range(2)
        ],
        axis=0,
    )
    final = dot(left, right).astype(jnp.bfloat16)
    rows = jnp.concatenate(
        [
            jnp.concatenate(
                [
                    final[
                        comp * inner + q * short : comp * inner + (q + 1) * short,
                        s * inner : (s + 1) * inner,
                    ]
                    for q in range(quad)
                ],
                axis=1,
            )
            for comp in range(2)
            for s in range(slabs)
        ],
        axis=0,
    )
    count = slabs * short
    load_groups.wait()
    spread = jnp.broadcast_to(groups_ref[...].astype(jnp.float32), (count, count))
    on_diagonal = lax.broadcasted_iota(jnp.int32, (count, count), 0)
    on_diagonal = on_diagonal == lax.broadcasted_iota(jnp.int32, (count, count), 1)
    named = jnp.sum(jnp.where(on_diagonal, spread, 0.0), axis=1, keepdims=True)
    real_sum = jnp.zeros(out_ref.shape[1:], jnp.float32)
    imag_sum = jnp.zeros(out_ref.shape[1:], jnp.float32)

    def project(group, real_sum, imag_sum):
        by_real = dot(rows, weights[group, 0])
        by_imag = dot(rows, weights[group, 1])
        here = named == group.astype(jnp.float32)
        real_sum = jnp.where(here, by_real[:count] - by_imag[count:], real_sum)
        imag_sum = jnp.where(here, by_imag[:count] + by_real[count:], imag_sum)
        return real_sum, imag_sum

    from_x(8)
    from_y(6)
    load_proj.wait()
    real_sum, imag_sum = project(home, real_sum, imag_sum)
    own.wait()
    real_sum, imag_sum = project(sibling, real_sum, imag_sum)
    real_sum, imag_sum = project(across, real_sum, imag_sum)
    for copy in over_core:
        copy.wait()
    real_sum, imag_sum = project(across_sibling, real_sum, imag_sum)
    for gain in [jnp.minimum(g, 1.0) for g in gains] + [jnp.maximum(g, 1.0) for g in gains]:
        real_sum = real_sum * gain
        imag_sum = imag_sum * gain
    out_ref[0] = real_sum.astype(jnp.bfloat16)
    out_ref[1] = imag_sum.astype(jnp.bfloat16)
    for copy in over_x:
        copy.wait_send()
    for copy in over_y:
        copy.wait_send()


def local(stem_state, branch_mats, branch_modes, out_proj, groups):
    slabs, inner = stem_state.shape[3], stem_state.shape[4]
    legs, branches = branch_mats.shape[:2]
    depth, out_len = out_proj.shape[2:]
    peers = lax.axis_size("modes")
    rows = slabs * inner
    row_total = rows * inner // depth
    part = rows // peers
    bf16 = jnp.bfloat16
    whole = pl.BlockSpec(memory_space=pl.ANY)
    result = pl.pallas_call(
        functools.partial(fused, (peers, legs, branches, slabs, inner, depth)),
        out_shape=jax.ShapeDtypeStruct((2, row_total, out_len), bf16),
        in_specs=[
            whole,
            whole,
            whole,
            whole,
            whole,
        ],
        out_specs=pl.BlockSpec(memory_space=pltpu.VMEM),
        scratch_shapes=[
            pltpu.SMEM(branch_modes.shape, jnp.int32),
            pltpu.VMEM((1, row_total), jnp.int32),
            pltpu.VMEM(branch_mats.shape, bf16),
            pltpu.VMEM((legs, branches + 1, inner, 2 * inner), bf16),
            pltpu.VMEM((peers, 2, part, inner), bf16),
            pltpu.VMEM((peers, part, 2 * inner), bf16),
            pltpu.VMEM((peers, part, 2 * inner), bf16),
            pltpu.VMEM((lax.axis_size("half"), 2, depth, out_len), bf16),
            pltpu.SemaphoreType.DMA((4 + legs,)),
            pltpu.SemaphoreType.DMA((WAVES, peers - 1)),
            pltpu.SemaphoreType.DMA((WAVES, peers - 1)),
            pltpu.SemaphoreType.DMA((WAVES, peers - 1)),
            pltpu.SemaphoreType.DMA((WAVES, peers - 1)),
            pltpu.SemaphoreType.DMA((DIRECT,)),
            pltpu.SemaphoreType.DMA((DIRECT,)),
            pltpu.SemaphoreType.DMA((CHUNKS - DIRECT,)),
            pltpu.SemaphoreType.DMA((CHUNKS - DIRECT,)),
            pltpu.SemaphoreType.DMA((1 + CHUNKS,)),
            pltpu.SemaphoreType.DMA((1 + CHUNKS,)),
        ],
        compiler_params=pltpu.CompilerParams(
            collective_id=0, has_side_effects=True, vmem_limit_bytes=60 * 1024 * 1024
        ),
    )(
        stem_state.reshape(2, rows, inner),
        branch_mats,
        branch_modes,
        out_proj.reshape(out_proj.shape[1:]),
        groups.reshape(1, row_total),
    )
    return result.reshape(1, 1, 2, row_total, out_len)


def solution(mesh):
    placed = (
        P(None, ("slices", "modes"), "half", None, None, None),
        P(),
        P(),
        P("half", None, None, None),
        P(("slices", "modes"), "half", None, None),
    )
    sizes = dict(mesh.shape)
    in_kernel = sizes["half"] == 4 and sizes["slices"] == 2 and sizes["modes"] <= 4
    return jax.shard_map(
        local if in_kernel else stepwise,
        mesh=mesh,
        in_specs=placed,
        out_specs=P(("slices", "modes"), "half", None, None, None),
        check_vma=False,
    )
```

```python
import functools

import jax
import jax.numpy as jnp
from jax import lax
from jax.experimental import pallas as pl
from jax.experimental.pallas import tpu as pltpu
from jax.sharding import PartitionSpec as P

MESH = pl.DeviceIdType.MESH
CHUNKS = 8
DIRECT = 5


def widen(matrix):
    real_part = matrix[0]
    imag_part = matrix[1]
    return jnp.stack([jnp.stack([real_part, imag_part]), jnp.stack([-imag_part, real_part])])


def contract_first(state, wide):
    value = jnp.einsum("isbc,ijbd->jsdc", state, wide, preferred_element_type=jnp.float32)
    return value.astype(jnp.bfloat16)


def contract_second(state, wide):
    value = jnp.einsum("isbc,ijcd->jsbd", state, wide, preferred_element_type=jnp.float32)
    return value.astype(jnp.bfloat16)


def stepwise(stem_state, branch_mats, branch_modes, out_proj, groups):
    slabs = stem_state.shape[3]
    inner = stem_state.shape[4]
    state = stem_state.reshape(2, slabs, inner, inner)
    peers = lax.axis_size("modes")
    width_part = inner // peers
    for leg in range(branch_mats.shape[0]):

        def advance(branch, current):
            wide = widen(branch_mats[leg][branch])
            return lax.cond(
                branch_modes[leg][branch] == 0, contract_first, contract_second, current, wide
            )

        state = lax.fori_loop(0, branch_mats.shape[1], advance, state)
        pieces = state.reshape(2, slabs, inner, peers, width_part)
        pieces = jnp.transpose(pieces, (3, 0, 1, 2, 4)).reshape(peers, 2, slabs, inner * width_part)
        pieces = lax.all_to_all(pieces, "modes", split_axis=0, concat_axis=0, tiled=True)
        pieces = pieces.reshape(peers, 2, slabs, inner, width_part)
        state = jnp.transpose(pieces, (1, 2, 3, 0, 4)).reshape(2, slabs, inner, inner)
    stem_len = out_proj.shape[2]
    out_len = out_proj.shape[3]
    row_total = slabs * inner * inner // stem_len
    rows = state.reshape(2, row_total, stem_len)
    chosen = groups.reshape(row_total)
    piece = lax.all_gather(out_proj, "half", axis=0, tiled=True)
    wides = jax.vmap(widen)(piece)
    product = jnp.einsum("irk,gijkd->gjrd", rows, wides, preferred_element_type=jnp.float32)
    owners = jnp.arange(piece.shape[0], dtype=jnp.int32)
    keep = chosen[None, :] == owners[:, None]
    products = jnp.where(keep[:, None, :, None], product, 0.0)
    result = jnp.sum(products, axis=0).astype(jnp.bfloat16)
    return result.reshape(1, 1, 2, row_total, out_len)


def dot(left, right):
    return jnp.dot(left, right, preferred_element_type=jnp.float32)


def wide_of(top):
    inner = top.shape[0]
    real_part, imag_part = top[:, :inner], top[:, inner:]
    return jnp.concatenate([top, jnp.concatenate([-imag_part, real_part], axis=1)], axis=0)


def normal(top):
    largest = jnp.max(jnp.abs(top), axis=(0, 1), keepdims=True)
    largest = jnp.where(largest > 0.0, largest, 1.0)
    return top * (1.0 / largest), largest


def fused(
    sizes,
    state_ref,
    mats_hbm,
    modes_hbm,
    proj_ref,
    groups_hbm,
    out_ref,
    modes_ref,
    groups_ref,
    mats,
    past,
    got,
    leave,
    back,
    weights,
    local_sem,
    first_send,
    first_recv,
    last_send,
    last_recv,
    x_send,
    x_recv,
    y_send,
    y_recv,
    core_send,
    core_recv,
):
    peers, legs, branches, slabs, inner, depth = sizes
    width = inner // peers
    me = lax.axis_index("modes")
    row = lax.axis_index("slices")
    home = lax.axis_index("half")
    core = lax.rem(home, 2)
    sibling = home + 1 - 2 * core
    across = lax.rem(home + 2, 4)
    across_sibling = lax.rem(sibling + 2, 4)
    other_row = 1 - row
    part = got.shape[2]
    piece = depth // CHUNKS
    handed = CHUNKS - DIRECT

    barrier = pltpu.get_barrier_semaphore()
    for step in range(1, peers):
        pl.semaphore_signal(
            barrier, inc=1, device_id={"modes": lax.rem(me + step, peers)}, device_id_type=MESH
        )
    pl.semaphore_signal(barrier, inc=1, device_id={"half": sibling}, device_id_type=MESH)
    pl.semaphore_signal(barrier, inc=1, device_id={"half": across}, device_id_type=MESH)
    pl.semaphore_signal(barrier, inc=1, device_id={"slices": other_row}, device_id_type=MESH)

    load_modes = pltpu.make_async_copy(modes_hbm, modes_ref, local_sem.at[0])
    load_modes.start()
    load_mats = []
    for leg in range(legs):
        load_mats.append(
            pltpu.make_async_copy(mats_hbm.at[leg], mats.at[leg], local_sem.at[4 + leg])
        )
        load_mats[leg].start()
    load_own = pltpu.make_async_copy(
        state_ref.at[:, pl.ds(me * part, part), :], got.at[me], local_sem.at[1]
    )
    load_own.start()
    pl.semaphore_wait(barrier, peers + 2)

    first = []
    for step in range(1, peers):
        target = lax.rem(me + step, peers)
        copy = pltpu.make_async_remote_copy(
            src_ref=state_ref.at[:, pl.ds(target * part, part), :],
            dst_ref=got.at[me],
            send_sem=first_send.at[step - 1],
            recv_sem=first_recv.at[step - 1],
            device_id={"modes": target},
            device_id_type=MESH,
        )
        copy.start()
        first.append(copy)

    def rows_of(which, chunk):
        forward = pl.multiple_of(which * (CHUNKS - 1) * piece + (1 - 2 * which) * chunk * piece, piece)
        return pl.ds(forward, piece)

    over_x, over_y, over_core = [], [], []
    for chunk in range(DIRECT):
        copy = pltpu.make_async_remote_copy(
            src_ref=proj_ref.at[:, rows_of(row, chunk), :],
            dst_ref=weights.at[home, :, rows_of(row, chunk), :],
            send_sem=x_send.at[chunk],
            recv_sem=x_recv.at[chunk],
            device_id={"half": across},
            device_id_type=MESH,
        )
        copy.start()
        over_x.append(copy)
    own = pltpu.make_async_remote_copy(
        src_ref=proj_ref,
        dst_ref=weights.at[home],
        send_sem=core_send.at[0],
        recv_sem=core_recv.at[0],
        device_id={"half": sibling},
        device_id_type=MESH,
    )
    load_proj = pltpu.make_async_copy(proj_ref, weights.at[home], local_sem.at[2])
    load_groups = pltpu.make_async_copy(groups_hbm, groups_ref, local_sem.at[3])

    def to_core(which, chunk, number):
        copy = pltpu.make_async_remote_copy(
            src_ref=weights.at[across, :, rows_of(which, chunk), :],
            dst_ref=weights.at[across, :, rows_of(which, chunk), :],
            send_sem=core_send.at[number],
            recv_sem=core_recv.at[number],
            device_id={"half": sibling},
            device_id_type=MESH,
        )
        copy.start()
        over_core.append(copy)

    def from_x(chunk):
        over_x[chunk].wait_recv()
        if chunk < handed:
            copy = pltpu.make_async_remote_copy(
                src_ref=weights.at[across, :, rows_of(row, chunk), :],
                dst_ref=weights.at[across, :, rows_of(row, chunk), :],
                send_sem=y_send.at[chunk],
                recv_sem=y_recv.at[chunk],
                device_id={"slices": other_row},
                device_id_type=MESH,
            )
            copy.start()
            over_y.append(copy)
        to_core(row, chunk, 1 + chunk)

    def from_y(chunk):
        over_y[chunk].wait_recv()
        to_core(other_row, chunk, 1 + DIRECT + chunk)

    load_modes.wait()
    lanes = lax.broadcasted_iota(jnp.int32, (inner, 2 * inner), 1)
    sublanes = lax.broadcasted_iota(jnp.int32, (inner, 2 * inner), 0)
    identity = jnp.where(lanes == sublanes, 1.0, 0.0).astype(jnp.bfloat16)
    last_b, last_c = {}, {}

    def start_leg(leg):
        load_mats[leg].wait()
        past[leg][0] = identity
        past[leg][1, :, :inner] = mats[leg, 0, 0]
        past[leg][1, :, inner:] = mats[leg, 0, 1]
        is_b = modes_ref[leg, 0] == 0
        last_b[leg] = jnp.where(is_b, 1, 0)
        last_c[leg] = jnp.where(is_b, 0, 1)

    def next_branch(leg, branch):
        is_b = modes_ref[leg, branch] == 0
        top = jnp.concatenate([mats[leg, branch, 0], mats[leg, branch, 1]], axis=1)
        before = past[leg][jnp.where(is_b, last_b[leg], last_c[leg])]
        past[leg][branch + 1] = dot(before, wide_of(top)).astype(jnp.bfloat16)
        last_b[leg] = jnp.where(is_b, branch + 1, last_b[leg])
        last_c[leg] = jnp.where(is_b, last_c[leg], branch + 1)

    block = lax.broadcasted_iota(jnp.int32, (part, inner), 1) // width

    def apply_leg(values, wide):
        product = dot(values, wide)
        swapped = []
        for m in range(peers):
            both = []
            for comp in range(2):
                taken = None
                for t in range(peers):
                    tile = product[t * part : (t + 1) * part, comp * inner : (comp + 1) * inner]
                    shift = (t - m) * width % inner
                    if shift:
                        tile = pltpu.roll(tile, shift, 1)
                    taken = tile if taken is None else jnp.where(block == t, tile, taken)
                both.append(taken)
            swapped.append(jnp.concatenate(both, axis=1))
        return jnp.concatenate(swapped, axis=0).astype(jnp.bfloat16)

    gains = []

    def scaled(top):
        top, gain = normal(top.astype(jnp.float32))
        gains.append(gain)
        return top.astype(jnp.bfloat16)

    early = min(2, legs)
    for leg in range(legs):
        start_leg(leg)
    for branch in range(1, branches):
        for leg in range(legs):
            next_branch(leg, branch)
    own.start()
    load_proj.start()
    load_groups.start()
    wides = []
    for leg in range(legs):
        top = past[leg][last_c[leg]]
        wides.append(wide_of(top if leg < early else scaled(top)))
    from_x(0)
    load_own.wait()
    for copy in first:
        copy.wait()
    values = jnp.concatenate(
        [jnp.concatenate([got[m, 0], got[m, 1]], axis=1) for m in range(peers)], axis=0
    )
    values = apply_leg(values, wides[0])
    from_x(1)
    for leg in range(1, legs - 1):
        values = apply_leg(values, wides[leg])
    from_x(2)
    values = apply_leg(values, wides[legs - 1])
    for m in range(peers):
        leave[m] = values[m * part : (m + 1) * part]

    last = []
    for step in range(1, peers):
        target = lax.rem(me + step, peers)
        copy = pltpu.make_async_remote_copy(
            src_ref=leave.at[target],
            dst_ref=back.at[me],
            send_sem=last_send.at[step - 1],
            recv_sem=last_recv.at[step - 1],
            device_id={"modes": target},
            device_id_type=MESH,
        )
        copy.start()
        last.append(copy)
    back[me] = leave[me]

    factors = [past[leg][last_b[leg]] for leg in range(legs)]
    while len(factors) > 1:
        pairs = [
            scaled(dot(factors[i], wide_of(factors[i + 1]))) for i in range(0, len(factors) - 1, 2)
        ]
        factors = pairs + factors[len(pairs) * 2 :]
    total = factors[0]
    stacked = jnp.concatenate([total[:, :inner], total[:, inner:]], axis=0)
    quad = depth // inner
    short = inner // quad
    target_row = lax.broadcasted_iota(jnp.int32, (inner, inner), 0)
    source_col = lax.broadcasted_iota(jnp.int32, (inner, inner), 1)
    order = (source_col % quad) * short + source_col // quad == target_row
    order = jnp.where(order, 1.0, 0.0).astype(jnp.bfloat16)
    turned = lax.dot_general(
        order, stacked, (((1,), (1,)), ((), ())), preferred_element_type=jnp.float32
    ).astype(jnp.bfloat16)
    real_part, imag_part = turned[:, :inner], turned[:, inner:]
    left = jnp.concatenate(
        [
            jnp.concatenate([real_part, -imag_part], axis=1),
            jnp.concatenate([imag_part, real_part], axis=1),
        ],
        axis=0,
    )
    from_y(0)
    from_x(3)
    from_y(1)
    from_x(4)
    from_y(2)

    for copy in last:
        copy.wait()
    arrived = jnp.concatenate([back[m] for m in range(peers)], axis=0)
    right = jnp.concatenate(
        [
            jnp.concatenate(
                [
                    arrived[s * inner : (s + 1) * inner, comp * inner : (comp + 1) * inner]
                    for s in range(slabs)
                ],
                axis=1,
            )
            for comp in range(2)
        ],
        axis=0,
    )
    final = dot(left, right).astype(jnp.bfloat16)
    rows = jnp.concatenate(
        [
            jnp.concatenate(
                [
                    final[
                        comp * inner + q * short : comp * inner + (q + 1) * short,
                        s * inner : (s + 1) * inner,
                    ]
                    for q in range(quad)
                ],
                axis=1,
            )
            for comp in range(2)
            for s in range(slabs)
        ],
        axis=0,
    )
    count = slabs * short
    load_groups.wait()
    spread = jnp.broadcast_to(groups_ref[...].astype(jnp.float32), (count, count))
    on_diagonal = lax.broadcasted_iota(jnp.int32, (count, count), 0)
    on_diagonal = on_diagonal == lax.broadcasted_iota(jnp.int32, (count, count), 1)
    named = jnp.sum(jnp.where(on_diagonal, spread, 0.0), axis=1, keepdims=True)
    real_sum = jnp.zeros(out_ref.shape[1:], jnp.float32)
    imag_sum = jnp.zeros(out_ref.shape[1:], jnp.float32)

    def project(group, real_sum, imag_sum):
        by_real = dot(rows, weights[group, 0])
        by_imag = dot(rows, weights[group, 1])
        here = named == group.astype(jnp.float32)
        real_sum = jnp.where(here, by_real[:count] - by_imag[count:], real_sum)
        imag_sum = jnp.where(here, by_imag[:count] + by_real[count:], imag_sum)
        return real_sum, imag_sum

    load_proj.wait()
    real_sum, imag_sum = project(home, real_sum, imag_sum)
    own.wait()
    real_sum, imag_sum = project(sibling, real_sum, imag_sum)
    real_sum, imag_sum = project(across, real_sum, imag_sum)
    for copy in over_core:
        copy.wait()
    real_sum, imag_sum = project(across_sibling, real_sum, imag_sum)
    for gain in [jnp.minimum(g, 1.0) for g in gains] + [jnp.maximum(g, 1.0) for g in gains]:
        real_sum = real_sum * gain
        imag_sum = imag_sum * gain
    out_ref[0] = real_sum.astype(jnp.bfloat16)
    out_ref[1] = imag_sum.astype(jnp.bfloat16)
    for copy in over_x:
        copy.wait_send()
    for copy in over_y:
        copy.wait_send()


def local(stem_state, branch_mats, branch_modes, out_proj, groups):
    slabs, inner = stem_state.shape[3], stem_state.shape[4]
    legs, branches = branch_mats.shape[:2]
    depth, out_len = out_proj.shape[2:]
    peers = lax.axis_size("modes")
    rows = slabs * inner
    row_total = rows * inner // depth
    part = rows // peers
    bf16 = jnp.bfloat16
    whole = pl.BlockSpec(memory_space=pl.ANY)
    result = pl.pallas_call(
        functools.partial(fused, (peers, legs, branches, slabs, inner, depth)),
        out_shape=jax.ShapeDtypeStruct((2, row_total, out_len), bf16),
        in_specs=[
            whole,
            whole,
            whole,
            whole,
            whole,
        ],
        out_specs=pl.BlockSpec(memory_space=pltpu.VMEM),
        scratch_shapes=[
            pltpu.SMEM(branch_modes.shape, jnp.int32),
            pltpu.VMEM((1, row_total), jnp.int32),
            pltpu.VMEM(branch_mats.shape, bf16),
            [pltpu.VMEM((branches + 1, inner, 2 * inner), bf16)] * legs,
            pltpu.VMEM((peers, 2, part, inner), bf16),
            pltpu.VMEM((peers, part, 2 * inner), bf16),
            pltpu.VMEM((peers, part, 2 * inner), bf16),
            pltpu.VMEM((lax.axis_size("half"), 2, depth, out_len), bf16),
            pltpu.SemaphoreType.DMA((4 + legs,)),
            pltpu.SemaphoreType.DMA((peers - 1,)),
            pltpu.SemaphoreType.DMA((peers - 1,)),
            pltpu.SemaphoreType.DMA((peers - 1,)),
            pltpu.SemaphoreType.DMA((peers - 1,)),
            pltpu.SemaphoreType.DMA((DIRECT,)),
            pltpu.SemaphoreType.DMA((DIRECT,)),
            pltpu.SemaphoreType.DMA((CHUNKS - DIRECT,)),
            pltpu.SemaphoreType.DMA((CHUNKS - DIRECT,)),
            pltpu.SemaphoreType.DMA((1 + CHUNKS,)),
            pltpu.SemaphoreType.DMA((1 + CHUNKS,)),
        ],
        compiler_params=pltpu.CompilerParams(
            collective_id=0, has_side_effects=True, vmem_limit_bytes=60 * 1024 * 1024
        ),
    )(
        stem_state.reshape(2, rows, inner),
        branch_mats,
        branch_modes,
        out_proj.reshape(out_proj.shape[1:]),
        groups.reshape(1, row_total),
    )
    return result.reshape(1, 1, 2, row_total, out_len)


def solution(mesh):
    placed = (
        P(None, ("slices", "modes"), "half", None, None, None),
        P(),
        P(),
        P("half", None, None, None),
        P(("slices", "modes"), "half", None, None),
    )
    sizes = dict(mesh.shape)
    in_kernel = sizes["half"] == 4 and sizes["slices"] == 2 and sizes["modes"] <= 4
    return jax.shard_map(
        local if in_kernel else stepwise,
        mesh=mesh,
        in_specs=placed,
        out_specs=P(("slices", "modes"), "half", None, None, None),
        check_vma=False,
    )
```

```python
import functools

import jax
import jax.numpy as jnp
from jax import lax
from jax.experimental import pallas as pl
from jax.experimental.pallas import tpu as pltpu
from jax.sharding import PartitionSpec as P

MESH = pl.DeviceIdType.MESH
CHUNKS = 8
DIRECT = 5
WAVES = 2


def widen(matrix):
    real_part = matrix[0]
    imag_part = matrix[1]
    return jnp.stack([jnp.stack([real_part, imag_part]), jnp.stack([-imag_part, real_part])])


def contract_first(state, wide):
    value = jnp.einsum("isbc,ijbd->jsdc", state, wide, preferred_element_type=jnp.float32)
    return value.astype(jnp.bfloat16)


def contract_second(state, wide):
    value = jnp.einsum("isbc,ijcd->jsbd", state, wide, preferred_element_type=jnp.float32)
    return value.astype(jnp.bfloat16)


def stepwise(stem_state, branch_mats, branch_modes, out_proj, groups):
    slabs = stem_state.shape[3]
    inner = stem_state.shape[4]
    state = stem_state.reshape(2, slabs, inner, inner)
    peers = lax.axis_size("modes")
    width_part = inner // peers
    for leg in range(branch_mats.shape[0]):

        def advance(branch, current):
            wide = widen(branch_mats[leg][branch])
            return lax.cond(
                branch_modes[leg][branch] == 0, contract_first, contract_second, current, wide
            )

        state = lax.fori_loop(0, branch_mats.shape[1], advance, state)
        pieces = state.reshape(2, slabs, inner, peers, width_part)
        pieces = jnp.transpose(pieces, (3, 0, 1, 2, 4)).reshape(peers, 2, slabs, inner * width_part)
        pieces = lax.all_to_all(pieces, "modes", split_axis=0, concat_axis=0, tiled=True)
        pieces = pieces.reshape(peers, 2, slabs, inner, width_part)
        state = jnp.transpose(pieces, (1, 2, 3, 0, 4)).reshape(2, slabs, inner, inner)
    stem_len = out_proj.shape[2]
    out_len = out_proj.shape[3]
    row_total = slabs * inner * inner // stem_len
    rows = state.reshape(2, row_total, stem_len)
    chosen = groups.reshape(row_total)
    piece = lax.all_gather(out_proj, "half", axis=0, tiled=True)
    wides = jax.vmap(widen)(piece)
    product = jnp.einsum("irk,gijkd->gjrd", rows, wides, preferred_element_type=jnp.float32)
    owners = jnp.arange(piece.shape[0], dtype=jnp.int32)
    keep = chosen[None, :] == owners[:, None]
    products = jnp.where(keep[:, None, :, None], product, 0.0)
    result = jnp.sum(products, axis=0).astype(jnp.bfloat16)
    return result.reshape(1, 1, 2, row_total, out_len)


def dot(left, right):
    return jnp.dot(left, right, preferred_element_type=jnp.float32)


def wide_of(top):
    inner = top.shape[0]
    real_part, imag_part = top[:, :inner], top[:, inner:]
    return jnp.concatenate([top, jnp.concatenate([-imag_part, real_part], axis=1)], axis=0)


def normal(top):
    largest = jnp.max(jnp.abs(top), axis=(0, 1), keepdims=True)
    largest = jnp.where(largest > 0.0, largest, 1.0)
    return top * (1.0 / largest), largest


def fused(
    sizes,
    state_ref,
    mats_hbm,
    modes_hbm,
    proj_ref,
    groups_hbm,
    out_ref,
    modes_ref,
    groups_ref,
    mats,
    past,
    got,
    leave,
    back,
    weights,
    local_sem,
    first_send,
    first_recv,
    last_send,
    last_recv,
    x_send,
    x_recv,
    y_send,
    y_recv,
    core_send,
    core_recv,
):
    peers, legs, branches, slabs, inner, depth = sizes
    width = inner // peers
    me = lax.axis_index("modes")
    row = lax.axis_index("slices")
    home = lax.axis_index("half")
    core = lax.rem(home, 2)
    sibling = home + 1 - 2 * core
    across = lax.rem(home + 2, 4)
    across_sibling = lax.rem(sibling + 2, 4)
    other_row = 1 - row
    part = got.shape[2]
    piece = depth // CHUNKS
    handed = CHUNKS - DIRECT

    barrier = pltpu.get_barrier_semaphore()
    for step in range(1, peers):
        pl.semaphore_signal(
            barrier, inc=1, device_id={"modes": lax.rem(me + step, peers)}, device_id_type=MESH
        )
    pl.semaphore_signal(barrier, inc=1, device_id={"half": sibling}, device_id_type=MESH)
    pl.semaphore_signal(barrier, inc=1, device_id={"half": across}, device_id_type=MESH)
    pl.semaphore_signal(barrier, inc=1, device_id={"slices": other_row}, device_id_type=MESH)

    load_modes = pltpu.make_async_copy(modes_hbm, modes_ref, local_sem.at[0])
    load_modes.start()
    load_mats = []
    for leg in range(legs):
        load_mats.append(
            pltpu.make_async_copy(mats_hbm.at[leg], mats.at[leg], local_sem.at[4 + leg])
        )
        load_mats[leg].start()
    load_own = pltpu.make_async_copy(
        state_ref.at[:, pl.ds(me * part, part), :], got.at[me], local_sem.at[1]
    )
    load_own.start()
    pl.semaphore_wait(barrier, peers + 2)

    stripe = part // WAVES
    first = []
    for wave in range(WAVES):
        for step in range(1, peers):
            target = lax.rem(me + step, peers)
            copy = pltpu.make_async_remote_copy(
                src_ref=state_ref.at[:, pl.ds(target * part + wave * stripe, stripe), :],
                dst_ref=got.at[me, :, pl.ds(wave * stripe, stripe), :],
                send_sem=first_send.at[wave, step - 1],
                recv_sem=first_recv.at[wave, step - 1],
                device_id={"modes": target},
                device_id_type=MESH,
            )
            copy.start()
            first.append(copy)

    def rows_of(which, chunk):
        forward = pl.multiple_of(which * (CHUNKS - 1) * piece + (1 - 2 * which) * chunk * piece, piece)
        return pl.ds(forward, piece)

    over_x, over_y, over_core = [], [], []
    for chunk in range(DIRECT):
        copy = pltpu.make_async_remote_copy(
            src_ref=proj_ref.at[:, rows_of(row, chunk), :],
            dst_ref=weights.at[home, :, rows_of(row, chunk), :],
            send_sem=x_send.at[chunk],
            recv_sem=x_recv.at[chunk],
            device_id={"half": across},
            device_id_type=MESH,
        )
        copy.start()
        over_x.append(copy)
    own = pltpu.make_async_remote_copy(
        src_ref=proj_ref,
        dst_ref=weights.at[home],
        send_sem=core_send.at[0],
        recv_sem=core_recv.at[0],
        device_id={"half": sibling},
        device_id_type=MESH,
    )
    load_proj = pltpu.make_async_copy(proj_ref, weights.at[home], local_sem.at[2])
    load_groups = pltpu.make_async_copy(groups_hbm, groups_ref, local_sem.at[3])

    def to_core(which, chunk, number):
        copy = pltpu.make_async_remote_copy(
            src_ref=weights.at[across, :, rows_of(which, chunk), :],
            dst_ref=weights.at[across, :, rows_of(which, chunk), :],
            send_sem=core_send.at[number],
            recv_sem=core_recv.at[number],
            device_id={"half": sibling},
            device_id_type=MESH,
        )
        copy.start()
        over_core.append(copy)

    def from_x(chunk):
        over_x[chunk].wait_recv()
        if chunk < handed:
            copy = pltpu.make_async_remote_copy(
                src_ref=weights.at[across, :, rows_of(row, chunk), :],
                dst_ref=weights.at[across, :, rows_of(row, chunk), :],
                send_sem=y_send.at[chunk],
                recv_sem=y_recv.at[chunk],
                device_id={"slices": other_row},
                device_id_type=MESH,
            )
            copy.start()
            over_y.append(copy)
        to_core(row, chunk, 1 + chunk)

    def from_y(chunk):
        over_y[chunk].wait_recv()
        to_core(other_row, chunk, 1 + DIRECT + chunk)

    load_modes.wait()
    lanes = lax.broadcasted_iota(jnp.int32, (inner, 2 * inner), 1)
    sublanes = lax.broadcasted_iota(jnp.int32, (inner, 2 * inner), 0)
    identity = jnp.where(lanes == sublanes, 1.0, 0.0).astype(jnp.bfloat16)
    last_b, last_c = {}, {}

    def start_leg(leg):
        load_mats[leg].wait()
        past[leg][0] = identity
        past[leg][1, :, :inner] = mats[leg, 0, 0]
        past[leg][1, :, inner:] = mats[leg, 0, 1]
        is_b = modes_ref[leg, 0] == 0
        last_b[leg] = jnp.where(is_b, 1, 0)
        last_c[leg] = jnp.where(is_b, 0, 1)

    def next_branch(leg, branch):
        is_b = modes_ref[leg, branch] == 0
        top = jnp.concatenate([mats[leg, branch, 0], mats[leg, branch, 1]], axis=1)
        before = past[leg][jnp.where(is_b, last_b[leg], last_c[leg])]
        past[leg][branch + 1] = dot(before, wide_of(top)).astype(jnp.bfloat16)
        last_b[leg] = jnp.where(is_b, branch + 1, last_b[leg])
        last_c[leg] = jnp.where(is_b, last_c[leg], branch + 1)

    block = lax.broadcasted_iota(jnp.int32, (stripe, inner), 1) // width

    def apply_leg(values, wide):
        product = dot(values, wide)
        swapped = []
        for m in range(peers):
            both = []
            for comp in range(2):
                taken = None
                for t in range(peers):
                    tile = product[t * stripe : (t + 1) * stripe, comp * inner : (comp + 1) * inner]
                    shift = (t - m) * width % inner
                    if shift:
                        tile = pltpu.roll(tile, shift, 1)
                    taken = tile if taken is None else jnp.where(block == t, tile, taken)
                both.append(taken)
            swapped.append(jnp.concatenate(both, axis=1))
        return jnp.concatenate(swapped, axis=0).astype(jnp.bfloat16)

    gains = []

    def scaled(top):
        top, gain = normal(top.astype(jnp.float32))
        gains.append(gain)
        return top.astype(jnp.bfloat16)

    early = min(2, legs)
    for leg in range(legs):
        start_leg(leg)
    for branch in range(1, branches):
        for leg in range(legs):
            next_branch(leg, branch)
    own.start()
    load_proj.start()
    load_groups.start()
    wides = []
    for leg in range(legs):
        top = past[leg][last_c[leg]]
        wides.append(wide_of(top if leg < early else scaled(top)))
    load_own.wait()
    last = []
    for wave in range(WAVES):
        strip = pl.ds(wave * stripe, stripe)
        for copy in first[wave * (peers - 1) : (wave + 1) * (peers - 1)]:
            copy.wait()
        from_x(wave)
        values = jnp.concatenate(
            [
                jnp.concatenate([got[m, 0, strip, :], got[m, 1, strip, :]], axis=1)
                for m in range(peers)
            ],
            axis=0,
        )
        for leg in range(legs):
            values = apply_leg(values, wides[leg])
        for m in range(peers):
            leave[m, strip, :] = values[m * stripe : (m + 1) * stripe]
        for step in range(1, peers):
            target = lax.rem(me + step, peers)
            copy = pltpu.make_async_remote_copy(
                src_ref=leave.at[target, strip, :],
                dst_ref=back.at[me, strip, :],
                send_sem=last_send.at[wave, step - 1],
                recv_sem=last_recv.at[wave, step - 1],
                device_id={"modes": target},
                device_id_type=MESH,
            )
            copy.start()
            last.append(copy)
    back[me] = leave[me]

    factors = [past[leg][last_b[leg]] for leg in range(legs)]
    while len(factors) > 1:
        pairs = [
            scaled(dot(factors[i], wide_of(factors[i + 1]))) for i in range(0, len(factors) - 1, 2)
        ]
        factors = pairs + factors[len(pairs) * 2 :]
    total = factors[0]
    stacked = jnp.concatenate([total[:, :inner], total[:, inner:]], axis=0)
    quad = depth // inner
    short = inner // quad
    target_row = lax.broadcasted_iota(jnp.int32, (inner, inner), 0)
    source_col = lax.broadcasted_iota(jnp.int32, (inner, inner), 1)
    order = (source_col % quad) * short + source_col // quad == target_row
    order = jnp.where(order, 1.0, 0.0).astype(jnp.bfloat16)
    turned = lax.dot_general(
        order, stacked, (((1,), (1,)), ((), ())), preferred_element_type=jnp.float32
    ).astype(jnp.bfloat16)
    real_part, imag_part = turned[:, :inner], turned[:, inner:]
    left = jnp.concatenate(
        [
            jnp.concatenate([real_part, -imag_part], axis=1),
            jnp.concatenate([imag_part, real_part], axis=1),
        ],
        axis=0,
    )
    for chunk in range(WAVES, DIRECT - 1):
        from_x(chunk)
        from_y(chunk - WAVES)

    for copy in last:
        copy.wait()
    arrived = jnp.concatenate([back[m] for m in range(peers)], axis=0)
    right = jnp.concatenate(
        [
            jnp.concatenate(
                [
                    arrived[s * inner : (s + 1) * inner, comp * inner : (comp + 1) * inner]
                    for s in range(slabs)
                ],
                axis=1,
            )
            for comp in range(2)
        ],
        axis=0,
    )
    final = dot(left, right).astype(jnp.bfloat16)
    rows = jnp.concatenate(
        [
            jnp.concatenate(
                [
                    final[
                        comp * inner + q * short : comp * inner + (q + 1) * short,
                        s * inner : (s + 1) * inner,
                    ]
                    for q in range(quad)
                ],
                axis=1,
            )
            for comp in range(2)
            for s in range(slabs)
        ],
        axis=0,
    )
    count = slabs * short
    load_groups.wait()
    spread = jnp.broadcast_to(groups_ref[...].astype(jnp.float32), (count, count))
    on_diagonal = lax.broadcasted_iota(jnp.int32, (count, count), 0)
    on_diagonal = on_diagonal == lax.broadcasted_iota(jnp.int32, (count, count), 1)
    named = jnp.sum(jnp.where(on_diagonal, spread, 0.0), axis=1, keepdims=True)
    real_sum = jnp.zeros(out_ref.shape[1:], jnp.float32)
    imag_sum = jnp.zeros(out_ref.shape[1:], jnp.float32)

    def project(group, real_sum, imag_sum):
        by_real = dot(rows, weights[group, 0])
        by_imag = dot(rows, weights[group, 1])
        here = named == group.astype(jnp.float32)
        real_sum = jnp.where(here, by_real[:count] - by_imag[count:], real_sum)
        imag_sum = jnp.where(here, by_imag[:count] + by_real[count:], imag_sum)
        return real_sum, imag_sum

    from_x(DIRECT - 1)
    for chunk in range(DIRECT - 1 - WAVES, handed):
        from_y(chunk)
    load_proj.wait()
    real_sum, imag_sum = project(home, real_sum, imag_sum)
    own.wait()
    real_sum, imag_sum = project(sibling, real_sum, imag_sum)
    real_sum, imag_sum = project(across, real_sum, imag_sum)
    for copy in over_core:
        copy.wait()
    real_sum, imag_sum = project(across_sibling, real_sum, imag_sum)
    for gain in [jnp.minimum(g, 1.0) for g in gains] + [jnp.maximum(g, 1.0) for g in gains]:
        real_sum = real_sum * gain
        imag_sum = imag_sum * gain
    out_ref[0] = real_sum.astype(jnp.bfloat16)
    out_ref[1] = imag_sum.astype(jnp.bfloat16)
    for copy in over_x:
        copy.wait_send()
    for copy in over_y:
        copy.wait_send()


def local(stem_state, branch_mats, branch_modes, out_proj, groups):
    slabs, inner = stem_state.shape[3], stem_state.shape[4]
    legs, branches = branch_mats.shape[:2]
    depth, out_len = out_proj.shape[2:]
    peers = lax.axis_size("modes")
    rows = slabs * inner
    row_total = rows * inner // depth
    part = rows // peers
    bf16 = jnp.bfloat16
    whole = pl.BlockSpec(memory_space=pl.ANY)
    result = pl.pallas_call(
        functools.partial(fused, (peers, legs, branches, slabs, inner, depth)),
        out_shape=jax.ShapeDtypeStruct((2, row_total, out_len), bf16),
        in_specs=[
            whole,
            whole,
            whole,
            whole,
            whole,
        ],
        out_specs=pl.BlockSpec(memory_space=pltpu.VMEM),
        scratch_shapes=[
            pltpu.SMEM(branch_modes.shape, jnp.int32),
            pltpu.VMEM((1, row_total), jnp.int32),
            pltpu.VMEM(branch_mats.shape, bf16),
            [pltpu.VMEM((branches + 1, inner, 2 * inner), bf16)] * legs,
            pltpu.VMEM((peers, 2, part, inner), bf16),
            pltpu.VMEM((peers, part, 2 * inner), bf16),
            pltpu.VMEM((peers, part, 2 * inner), bf16),
            pltpu.VMEM((lax.axis_size("half"), 2, depth, out_len), bf16),
            pltpu.SemaphoreType.DMA((4 + legs,)),
            pltpu.SemaphoreType.DMA((WAVES, peers - 1)),
            pltpu.SemaphoreType.DMA((WAVES, peers - 1)),
            pltpu.SemaphoreType.DMA((WAVES, peers - 1)),
            pltpu.SemaphoreType.DMA((WAVES, peers - 1)),
            pltpu.SemaphoreType.DMA((DIRECT,)),
            pltpu.SemaphoreType.DMA((DIRECT,)),
            pltpu.SemaphoreType.DMA((CHUNKS - DIRECT,)),
            pltpu.SemaphoreType.DMA((CHUNKS - DIRECT,)),
            pltpu.SemaphoreType.DMA((1 + CHUNKS,)),
            pltpu.SemaphoreType.DMA((1 + CHUNKS,)),
        ],
        compiler_params=pltpu.CompilerParams(
            collective_id=0, has_side_effects=True, vmem_limit_bytes=60 * 1024 * 1024
        ),
    )(
        stem_state.reshape(2, rows, inner),
        branch_mats,
        branch_modes,
        out_proj.reshape(out_proj.shape[1:]),
        groups.reshape(1, row_total),
    )
    return result.reshape(1, 1, 2, row_total, out_len)


def solution(mesh):
    placed = (
        P(None, ("slices", "modes"), "half", None, None, None),
        P(),
        P(),
        P("half", None, None, None),
        P(("slices", "modes"), "half", None, None),
    )
    sizes = dict(mesh.shape)
    in_kernel = sizes["half"] == 4 and sizes["slices"] == 2 and sizes["modes"] <= 4
    return jax.shard_map(
        local if in_kernel else stepwise,
        mesh=mesh,
        in_specs=placed,
        out_specs=P(("slices", "modes"), "half", None, None, None),
        check_vma=False,
    )
```

```python
import functools

import jax
import jax.numpy as jnp
from jax import lax
from jax.experimental import pallas as pl
from jax.experimental.pallas import tpu as pltpu
from jax.sharding import PartitionSpec as P

MESH = pl.DeviceIdType.MESH
CHUNKS = 8
DIRECT = 5
WAVES = 2


def widen(matrix):
    real_part = matrix[0]
    imag_part = matrix[1]
    return jnp.stack([jnp.stack([real_part, imag_part]), jnp.stack([-imag_part, real_part])])


def contract_first(state, wide):
    value = jnp.einsum("isbc,ijbd->jsdc", state, wide, preferred_element_type=jnp.float32)
    return value.astype(jnp.bfloat16)


def contract_second(state, wide):
    value = jnp.einsum("isbc,ijcd->jsbd", state, wide, preferred_element_type=jnp.float32)
    return value.astype(jnp.bfloat16)


def stepwise(stem_state, branch_mats, branch_modes, out_proj, groups):
    slabs = stem_state.shape[3]
    inner = stem_state.shape[4]
    state = stem_state.reshape(2, slabs, inner, inner)
    peers = lax.axis_size("modes")
    width_part = inner // peers
    for leg in range(branch_mats.shape[0]):

        def advance(branch, current):
            wide = widen(branch_mats[leg][branch])
            return lax.cond(
                branch_modes[leg][branch] == 0, contract_first, contract_second, current, wide
            )

        state = lax.fori_loop(0, branch_mats.shape[1], advance, state)
        pieces = state.reshape(2, slabs, inner, peers, width_part)
        pieces = jnp.transpose(pieces, (3, 0, 1, 2, 4)).reshape(peers, 2, slabs, inner * width_part)
        pieces = lax.all_to_all(pieces, "modes", split_axis=0, concat_axis=0, tiled=True)
        pieces = pieces.reshape(peers, 2, slabs, inner, width_part)
        state = jnp.transpose(pieces, (1, 2, 3, 0, 4)).reshape(2, slabs, inner, inner)
    stem_len = out_proj.shape[2]
    out_len = out_proj.shape[3]
    row_total = slabs * inner * inner // stem_len
    rows = state.reshape(2, row_total, stem_len)
    chosen = groups.reshape(row_total)
    piece = lax.all_gather(out_proj, "half", axis=0, tiled=True)
    wides = jax.vmap(widen)(piece)
    product = jnp.einsum("irk,gijkd->gjrd", rows, wides, preferred_element_type=jnp.float32)
    owners = jnp.arange(piece.shape[0], dtype=jnp.int32)
    keep = chosen[None, :] == owners[:, None]
    products = jnp.where(keep[:, None, :, None], product, 0.0)
    result = jnp.sum(products, axis=0).astype(jnp.bfloat16)
    return result.reshape(1, 1, 2, row_total, out_len)


def dot(left, right):
    return jnp.dot(left, right, preferred_element_type=jnp.float32)


def wide_of(top):
    inner = top.shape[0]
    real_part, imag_part = top[:, :inner], top[:, inner:]
    return jnp.concatenate([top, jnp.concatenate([-imag_part, real_part], axis=1)], axis=0)


def normal(top):
    largest = jnp.max(jnp.abs(top), axis=(0, 1), keepdims=True)
    largest = jnp.where(largest > 0.0, largest, 1.0)
    return top * (1.0 / largest), largest


def fused(
    sizes,
    state_ref,
    mats_hbm,
    modes_hbm,
    proj_ref,
    groups_hbm,
    out_ref,
    modes_ref,
    groups_ref,
    mats,
    past,
    got,
    leave,
    back,
    weights,
    local_sem,
    first_send,
    first_recv,
    last_send,
    last_recv,
    x_send,
    x_recv,
    y_send,
    y_recv,
    core_send,
    core_recv,
):
    peers, legs, branches, slabs, inner, depth = sizes
    width = inner // peers
    me = lax.axis_index("modes")
    row = lax.axis_index("slices")
    home = lax.axis_index("half")
    core = lax.rem(home, 2)
    sibling = home + 1 - 2 * core
    across = lax.rem(home + 2, 4)
    across_sibling = lax.rem(sibling + 2, 4)
    other_row = 1 - row
    part = got.shape[2]
    piece = depth // CHUNKS
    handed = CHUNKS - DIRECT

    barrier = pltpu.get_barrier_semaphore()
    for step in range(1, peers):
        pl.semaphore_signal(
            barrier, inc=1, device_id={"modes": lax.rem(me + step, peers)}, device_id_type=MESH
        )
    pl.semaphore_signal(barrier, inc=1, device_id={"half": sibling}, device_id_type=MESH)
    pl.semaphore_signal(barrier, inc=1, device_id={"half": across}, device_id_type=MESH)
    pl.semaphore_signal(barrier, inc=1, device_id={"slices": other_row}, device_id_type=MESH)

    load_modes = pltpu.make_async_copy(modes_hbm, modes_ref, local_sem.at[0])
    load_modes.start()
    load_mats = []
    for leg in range(legs):
        load_mats.append(
            pltpu.make_async_copy(mats_hbm.at[leg], mats.at[leg], local_sem.at[4 + leg])
        )
        load_mats[leg].start()
    load_own = pltpu.make_async_copy(
        state_ref.at[:, pl.ds(me * part, part), :], got.at[me], local_sem.at[1]
    )
    load_own.start()
    pl.semaphore_wait(barrier, peers + 2)

    def rows_of(which, chunk):
        forward = pl.multiple_of(which * (CHUNKS - 1) * piece + (1 - 2 * which) * chunk * piece, piece)
        return pl.ds(forward, piece)

    over_x, over_y, over_core = [], [], []
    for chunk in range(DIRECT):
        copy = pltpu.make_async_remote_copy(
            src_ref=proj_ref.at[:, rows_of(row, chunk), :],
            dst_ref=weights.at[home, :, rows_of(row, chunk), :],
            send_sem=x_send.at[chunk],
            recv_sem=x_recv.at[chunk],
            device_id={"half": across},
            device_id_type=MESH,
        )
        copy.start()
        over_x.append(copy)
    stripe = part // WAVES
    first = []
    for wave in range(WAVES):
        for step in range(1, peers):
            target = lax.rem(me + step, peers)
            copy = pltpu.make_async_remote_copy(
                src_ref=state_ref.at[:, pl.ds(target * part + wave * stripe, stripe), :],
                dst_ref=got.at[me, :, pl.ds(wave * stripe, stripe), :],
                send_sem=first_send.at[wave, step - 1],
                recv_sem=first_recv.at[wave, step - 1],
                device_id={"modes": target},
                device_id_type=MESH,
            )
            copy.start()
            first.append(copy)

    own = pltpu.make_async_remote_copy(
        src_ref=proj_ref,
        dst_ref=weights.at[home],
        send_sem=core_send.at[0],
        recv_sem=core_recv.at[0],
        device_id={"half": sibling},
        device_id_type=MESH,
    )
    load_proj = pltpu.make_async_copy(proj_ref, weights.at[home], local_sem.at[2])
    load_groups = pltpu.make_async_copy(groups_hbm, groups_ref, local_sem.at[3])

    def to_core(which, chunk, number):
        copy = pltpu.make_async_remote_copy(
            src_ref=weights.at[across, :, rows_of(which, chunk), :],
            dst_ref=weights.at[across, :, rows_of(which, chunk), :],
            send_sem=core_send.at[number],
            recv_sem=core_recv.at[number],
            device_id={"half": sibling},
            device_id_type=MESH,
        )
        copy.start()
        over_core.append(copy)

    def from_x(chunk):
        over_x[chunk].wait_recv()
        if chunk < handed:
            copy = pltpu.make_async_remote_copy(
                src_ref=weights.at[across, :, rows_of(row, chunk), :],
                dst_ref=weights.at[across, :, rows_of(row, chunk), :],
                send_sem=y_send.at[chunk],
                recv_sem=y_recv.at[chunk],
                device_id={"slices": other_row},
                device_id_type=MESH,
            )
            copy.start()
            over_y.append(copy)
        to_core(row, chunk, 1 + chunk)

    def from_y(chunk):
        over_y[chunk].wait_recv()
        to_core(other_row, chunk, 1 + DIRECT + chunk)

    load_modes.wait()
    lanes = lax.broadcasted_iota(jnp.int32, (inner, 2 * inner), 1)
    sublanes = lax.broadcasted_iota(jnp.int32, (inner, 2 * inner), 0)
    identity = jnp.where(lanes == sublanes, 1.0, 0.0).astype(jnp.bfloat16)
    last_b, last_c = {}, {}

    def start_leg(leg):
        load_mats[leg].wait()
        past[leg][0] = identity
        past[leg][1, :, :inner] = mats[leg, 0, 0]
        past[leg][1, :, inner:] = mats[leg, 0, 1]
        is_b = modes_ref[leg, 0] == 0
        last_b[leg] = jnp.where(is_b, 1, 0)
        last_c[leg] = jnp.where(is_b, 0, 1)

    def next_branch(leg, branch):
        is_b = modes_ref[leg, branch] == 0
        top = jnp.concatenate([mats[leg, branch, 0], mats[leg, branch, 1]], axis=1)
        before = past[leg][jnp.where(is_b, last_b[leg], last_c[leg])]
        past[leg][branch + 1] = dot(before, wide_of(top)).astype(jnp.bfloat16)
        last_b[leg] = jnp.where(is_b, branch + 1, last_b[leg])
        last_c[leg] = jnp.where(is_b, last_c[leg], branch + 1)

    block = lax.broadcasted_iota(jnp.int32, (stripe, inner), 1) // width

    def apply_leg(values, wide):
        product = dot(values, wide)
        swapped = []
        for m in range(peers):
            both = []
            for comp in range(2):
                taken = None
                for t in range(peers):
                    tile = product[t * stripe : (t + 1) * stripe, comp * inner : (comp + 1) * inner]
                    shift = (t - m) * width % inner
                    if shift:
                        tile = pltpu.roll(tile, shift, 1)
                    taken = tile if taken is None else jnp.where(block == t, tile, taken)
                both.append(taken)
            swapped.append(jnp.concatenate(both, axis=1))
        return jnp.concatenate(swapped, axis=0).astype(jnp.bfloat16)

    gains = []

    def scaled(top):
        top, gain = normal(top.astype(jnp.float32))
        gains.append(gain)
        return top.astype(jnp.bfloat16)

    early = min(2, legs)
    for leg in range(legs):
        start_leg(leg)
    for branch in range(1, branches):
        for leg in range(legs):
            next_branch(leg, branch)
    own.start()
    load_proj.start()
    load_groups.start()
    wides = []
    for leg in range(legs):
        top = past[leg][last_c[leg]]
        wides.append(wide_of(top if leg < early else scaled(top)))
    from_x(0)
    load_own.wait()
    last = []
    for wave in range(WAVES):
        strip = pl.ds(wave * stripe, stripe)
        for copy in first[wave * (peers - 1) : (wave + 1) * (peers - 1)]:
            copy.wait()
        values = jnp.concatenate(
            [
                jnp.concatenate([got[m, 0, strip, :], got[m, 1, strip, :]], axis=1)
                for m in range(peers)
            ],
            axis=0,
        )
        for leg in range(legs):
            values = apply_leg(values, wides[leg])
            if wave == WAVES - 1 and leg == 0:
                from_x(2)
        for m in range(peers):
            leave[m, strip, :] = values[m * stripe : (m + 1) * stripe]
        for step in range(1, peers):
            target = lax.rem(me + step, peers)
            copy = pltpu.make_async_remote_copy(
                src_ref=leave.at[target, strip, :],
                dst_ref=back.at[me, strip, :],
                send_sem=last_send.at[wave, step - 1],
                recv_sem=last_recv.at[wave, step - 1],
                device_id={"modes": target},
                device_id_type=MESH,
            )
            copy.start()
            last.append(copy)
        if wave == 0:
            from_x(1)
    back[me] = leave[me]

    factors = [past[leg][last_b[leg]] for leg in range(legs)]
    while len(factors) > 1:
        pairs = [
            scaled(dot(factors[i], wide_of(factors[i + 1]))) for i in range(0, len(factors) - 1, 2)
        ]
        factors = pairs + factors[len(pairs) * 2 :]
    total = factors[0]
    stacked = jnp.concatenate([total[:, :inner], total[:, inner:]], axis=0)
    quad = depth // inner
    short = inner // quad
    target_row = lax.broadcasted_iota(jnp.int32, (inner, inner), 0)
    source_col = lax.broadcasted_iota(jnp.int32, (inner, inner), 1)
    order = (source_col % quad) * short + source_col // quad == target_row
    order = jnp.where(order, 1.0, 0.0).astype(jnp.bfloat16)
    turned = lax.dot_general(
        order, stacked, (((1,), (1,)), ((), ())), preferred_element_type=jnp.float32
    ).astype(jnp.bfloat16)
    real_part, imag_part = turned[:, :inner], turned[:, inner:]
    left = jnp.concatenate(
        [
            jnp.concatenate([real_part, -imag_part], axis=1),
            jnp.concatenate([imag_part, real_part], axis=1),
        ],
        axis=0,
    )
    for chunk in range(handed):
        from_y(chunk)
        if chunk + handed < DIRECT:
            from_x(chunk + handed)

    for copy in last:
        copy.wait()
    arrived = jnp.concatenate([back[m] for m in range(peers)], axis=0)
    right = jnp.concatenate(
        [
            jnp.concatenate(
                [
                    arrived[s * inner : (s + 1) * inner, comp * inner : (comp + 1) * inner]
                    for s in range(slabs)
                ],
                axis=1,
            )
            for comp in range(2)
        ],
        axis=0,
    )
    final = dot(left, right).astype(jnp.bfloat16)
    rows = jnp.concatenate(
        [
            jnp.concatenate(
                [
                    final[
                        comp * inner + q * short : comp * inner + (q + 1) * short,
                        s * inner : (s + 1) * inner,
                    ]
                    for q in range(quad)
                ],
                axis=1,
            )
            for comp in range(2)
            for s in range(slabs)
        ],
        axis=0,
    )
    count = slabs * short
    load_groups.wait()
    spread = jnp.broadcast_to(groups_ref[...].astype(jnp.float32), (count, count))
    on_diagonal = lax.broadcasted_iota(jnp.int32, (count, count), 0)
    on_diagonal = on_diagonal == lax.broadcasted_iota(jnp.int32, (count, count), 1)
    named = jnp.sum(jnp.where(on_diagonal, spread, 0.0), axis=1, keepdims=True)
    real_sum = jnp.zeros(out_ref.shape[1:], jnp.float32)
    imag_sum = jnp.zeros(out_ref.shape[1:], jnp.float32)

    def project(group, real_sum, imag_sum):
        by_real = dot(rows, weights[group, 0])
        by_imag = dot(rows, weights[group, 1])
        here = named == group.astype(jnp.float32)
        real_sum = jnp.where(here, by_real[:count] - by_imag[count:], real_sum)
        imag_sum = jnp.where(here, by_imag[:count] + by_real[count:], imag_sum)
        return real_sum, imag_sum

    load_proj.wait()
    real_sum, imag_sum = project(home, real_sum, imag_sum)
    own.wait()
    real_sum, imag_sum = project(sibling, real_sum, imag_sum)
    real_sum, imag_sum = project(across, real_sum, imag_sum)
    for copy in over_core:
        copy.wait()
    real_sum, imag_sum = project(across_sibling, real_sum, imag_sum)
    for gain in [jnp.minimum(g, 1.0) for g in gains] + [jnp.maximum(g, 1.0) for g in gains]:
        real_sum = real_sum * gain
        imag_sum = imag_sum * gain
    out_ref[0] = real_sum.astype(jnp.bfloat16)
    out_ref[1] = imag_sum.astype(jnp.bfloat16)
    for copy in over_x:
        copy.wait_send()
    for copy in over_y:
        copy.wait_send()


def local(stem_state, branch_mats, branch_modes, out_proj, groups):
    slabs, inner = stem_state.shape[3], stem_state.shape[4]
    legs, branches = branch_mats.shape[:2]
    depth, out_len = out_proj.shape[2:]
    peers = lax.axis_size("modes")
    rows = slabs * inner
    row_total = rows * inner // depth
    part = rows // peers
    bf16 = jnp.bfloat16
    whole = pl.BlockSpec(memory_space=pl.ANY)
    result = pl.pallas_call(
        functools.partial(fused, (peers, legs, branches, slabs, inner, depth)),
        out_shape=jax.ShapeDtypeStruct((2, row_total, out_len), bf16),
        in_specs=[
            whole,
            whole,
            whole,
            whole,
            whole,
        ],
        out_specs=pl.BlockSpec(memory_space=pltpu.VMEM),
        scratch_shapes=[
            pltpu.SMEM(branch_modes.shape, jnp.int32),
            pltpu.VMEM((1, row_total), jnp.int32),
            pltpu.VMEM(branch_mats.shape, bf16),
            [pltpu.VMEM((branches + 1, inner, 2 * inner), bf16)] * legs,
            pltpu.VMEM((peers, 2, part, inner), bf16),
            pltpu.VMEM((peers, part, 2 * inner), bf16),
            pltpu.VMEM((peers, part, 2 * inner), bf16),
            pltpu.VMEM((lax.axis_size("half"), 2, depth, out_len), bf16),
            pltpu.SemaphoreType.DMA((4 + legs,)),
            pltpu.SemaphoreType.DMA((WAVES, peers - 1)),
            pltpu.SemaphoreType.DMA((WAVES, peers - 1)),
            pltpu.SemaphoreType.DMA((WAVES, peers - 1)),
            pltpu.SemaphoreType.DMA((WAVES, peers - 1)),
            pltpu.SemaphoreType.DMA((DIRECT,)),
            pltpu.SemaphoreType.DMA((DIRECT,)),
            pltpu.SemaphoreType.DMA((CHUNKS - DIRECT,)),
            pltpu.SemaphoreType.DMA((CHUNKS - DIRECT,)),
            pltpu.SemaphoreType.DMA((1 + CHUNKS,)),
            pltpu.SemaphoreType.DMA((1 + CHUNKS,)),
        ],
        compiler_params=pltpu.CompilerParams(
            collective_id=0, has_side_effects=True, vmem_limit_bytes=60 * 1024 * 1024
        ),
    )(
        stem_state.reshape(2, rows, inner),
        branch_mats,
        branch_modes,
        out_proj.reshape(out_proj.shape[1:]),
        groups.reshape(1, row_total),
    )
    return result.reshape(1, 1, 2, row_total, out_len)


def solution(mesh):
    placed = (
        P(None, ("slices", "modes"), "half", None, None, None),
        P(),
        P(),
        P("half", None, None, None),
        P(("slices", "modes"), "half", None, None),
    )
    sizes = dict(mesh.shape)
    in_kernel = sizes["half"] == 4 and sizes["slices"] == 2 and sizes["modes"] <= 4
    return jax.shard_map(
        local if in_kernel else stepwise,
        mesh=mesh,
        in_specs=placed,
        out_specs=P(("slices", "modes"), "half", None, None, None),
        check_vma=False,
    )
```

```python
import functools

import jax
import jax.numpy as jnp
from jax import lax
from jax.experimental import pallas as pl
from jax.experimental.pallas import tpu as pltpu
from jax.sharding import PartitionSpec as P

MESH = pl.DeviceIdType.MESH
CHUNKS = 8
DIRECT = 5
WAVES = 2


def widen(matrix):
    real_part = matrix[0]
    imag_part = matrix[1]
    return jnp.stack([jnp.stack([real_part, imag_part]), jnp.stack([-imag_part, real_part])])


def contract_first(state, wide):
    value = jnp.einsum("isbc,ijbd->jsdc", state, wide, preferred_element_type=jnp.float32)
    return value.astype(jnp.bfloat16)


def contract_second(state, wide):
    value = jnp.einsum("isbc,ijcd->jsbd", state, wide, preferred_element_type=jnp.float32)
    return value.astype(jnp.bfloat16)


def stepwise(stem_state, branch_mats, branch_modes, out_proj, groups):
    slabs = stem_state.shape[3]
    inner = stem_state.shape[4]
    state = stem_state.reshape(2, slabs, inner, inner)
    peers = lax.axis_size("modes")
    width_part = inner // peers
    for leg in range(branch_mats.shape[0]):

        def advance(branch, current):
            wide = widen(branch_mats[leg][branch])
            return lax.cond(
                branch_modes[leg][branch] == 0, contract_first, contract_second, current, wide
            )

        state = lax.fori_loop(0, branch_mats.shape[1], advance, state)
        pieces = state.reshape(2, slabs, inner, peers, width_part)
        pieces = jnp.transpose(pieces, (3, 0, 1, 2, 4)).reshape(peers, 2, slabs, inner * width_part)
        pieces = lax.all_to_all(pieces, "modes", split_axis=0, concat_axis=0, tiled=True)
        pieces = pieces.reshape(peers, 2, slabs, inner, width_part)
        state = jnp.transpose(pieces, (1, 2, 3, 0, 4)).reshape(2, slabs, inner, inner)
    stem_len = out_proj.shape[2]
    out_len = out_proj.shape[3]
    row_total = slabs * inner * inner // stem_len
    rows = state.reshape(2, row_total, stem_len)
    chosen = groups.reshape(row_total)
    piece = lax.all_gather(out_proj, "half", axis=0, tiled=True)
    wides = jax.vmap(widen)(piece)
    product = jnp.einsum("irk,gijkd->gjrd", rows, wides, preferred_element_type=jnp.float32)
    owners = jnp.arange(piece.shape[0], dtype=jnp.int32)
    keep = chosen[None, :] == owners[:, None]
    products = jnp.where(keep[:, None, :, None], product, 0.0)
    result = jnp.sum(products, axis=0).astype(jnp.bfloat16)
    return result.reshape(1, 1, 2, row_total, out_len)


def dot(left, right):
    return jnp.dot(left, right, preferred_element_type=jnp.float32)


def wide_of(top):
    inner = top.shape[0]
    real_part, imag_part = top[:, :inner], top[:, inner:]
    return jnp.concatenate([top, jnp.concatenate([-imag_part, real_part], axis=1)], axis=0)


def normal(top):
    largest = jnp.max(jnp.abs(top), axis=(0, 1), keepdims=True)
    largest = jnp.where(largest > 0.0, largest, 1.0)
    return top * (1.0 / largest), largest


def fused(
    sizes,
    state_ref,
    mats_hbm,
    modes_hbm,
    proj_ref,
    groups_hbm,
    out_ref,
    modes_ref,
    groups_ref,
    mats,
    past,
    got,
    leave,
    back,
    weights,
    local_sem,
    first_send,
    first_recv,
    last_send,
    last_recv,
    x_send,
    x_recv,
    y_send,
    y_recv,
    core_send,
    core_recv,
):
    peers, legs, branches, slabs, inner, depth = sizes
    width = inner // peers
    me = lax.axis_index("modes")
    row = lax.axis_index("slices")
    home = lax.axis_index("half")
    core = lax.rem(home, 2)
    sibling = home + 1 - 2 * core
    across = lax.rem(home + 2, 4)
    across_sibling = lax.rem(sibling + 2, 4)
    other_row = 1 - row
    part = got.shape[2]
    piece = depth // CHUNKS
    handed = CHUNKS - DIRECT

    barrier = pltpu.get_barrier_semaphore()
    for step in range(1, peers):
        pl.semaphore_signal(
            barrier, inc=1, device_id={"modes": lax.rem(me + step, peers)}, device_id_type=MESH
        )
    pl.semaphore_signal(barrier, inc=1, device_id={"half": sibling}, device_id_type=MESH)
    pl.semaphore_signal(barrier, inc=1, device_id={"half": across}, device_id_type=MESH)
    pl.semaphore_signal(barrier, inc=1, device_id={"slices": other_row}, device_id_type=MESH)

    load_modes = pltpu.make_async_copy(modes_hbm, modes_ref, local_sem.at[0])
    load_modes.start()
    load_mats = []
    for leg in range(legs):
        load_mats.append(
            pltpu.make_async_copy(mats_hbm.at[leg], mats.at[leg], local_sem.at[4 + leg])
        )
        load_mats[leg].start()
    load_own = pltpu.make_async_copy(
        state_ref.at[:, pl.ds(me * part, part), :], got.at[me], local_sem.at[1]
    )
    load_own.start()
    pl.semaphore_wait(barrier, peers + 2)

    def rows_of(which, chunk):
        forward = pl.multiple_of(which * (CHUNKS - 1) * piece + (1 - 2 * which) * chunk * piece, piece)
        return pl.ds(forward, piece)

    over_x, over_y, over_core = [], [], []
    for chunk in range(DIRECT):
        copy = pltpu.make_async_remote_copy(
            src_ref=proj_ref.at[:, rows_of(row, chunk), :],
            dst_ref=weights.at[home, :, rows_of(row, chunk), :],
            send_sem=x_send.at[chunk],
            recv_sem=x_recv.at[chunk],
            device_id={"half": across},
            device_id_type=MESH,
        )
        copy.start()
        over_x.append(copy)
    stripe = part // WAVES
    first = []
    for wave in range(WAVES):
        for step in range(1, peers):
            target = lax.rem(me + step, peers)
            copy = pltpu.make_async_remote_copy(
                src_ref=state_ref.at[:, pl.ds(target * part + wave * stripe, stripe), :],
                dst_ref=got.at[me, :, pl.ds(wave * stripe, stripe), :],
                send_sem=first_send.at[wave, step - 1],
                recv_sem=first_recv.at[wave, step - 1],
                device_id={"modes": target},
                device_id_type=MESH,
            )
            copy.start()
            first.append(copy)

    own = pltpu.make_async_remote_copy(
        src_ref=proj_ref,
        dst_ref=weights.at[home],
        send_sem=core_send.at[0],
        recv_sem=core_recv.at[0],
        device_id={"half": sibling},
        device_id_type=MESH,
    )
    load_proj = pltpu.make_async_copy(proj_ref, weights.at[home], local_sem.at[2])
    load_groups = pltpu.make_async_copy(groups_hbm, groups_ref, local_sem.at[3])

    def to_core(which, chunk, number):
        copy = pltpu.make_async_remote_copy(
            src_ref=weights.at[across, :, rows_of(which, chunk), :],
            dst_ref=weights.at[across, :, rows_of(which, chunk), :],
            send_sem=core_send.at[number],
            recv_sem=core_recv.at[number],
            device_id={"half": sibling},
            device_id_type=MESH,
        )
        copy.start()
        over_core.append(copy)

    def from_x(chunk):
        over_x[chunk].wait_recv()
        if chunk < handed:
            copy = pltpu.make_async_remote_copy(
                src_ref=weights.at[across, :, rows_of(row, chunk), :],
                dst_ref=weights.at[across, :, rows_of(row, chunk), :],
                send_sem=y_send.at[chunk],
                recv_sem=y_recv.at[chunk],
                device_id={"slices": other_row},
                device_id_type=MESH,
            )
            copy.start()
            over_y.append(copy)
        to_core(row, chunk, 1 + chunk)

    def from_y(chunk):
        over_y[chunk].wait_recv()
        to_core(other_row, chunk, 1 + DIRECT + chunk)

    load_modes.wait()
    lanes = lax.broadcasted_iota(jnp.int32, (inner, 2 * inner), 1)
    sublanes = lax.broadcasted_iota(jnp.int32, (inner, 2 * inner), 0)
    identity = jnp.where(lanes == sublanes, 1.0, 0.0).astype(jnp.bfloat16)
    last_b, last_c = {}, {}

    def start_leg(leg):
        load_mats[leg].wait()
        past[leg][0] = identity
        past[leg][1, :, :inner] = mats[leg, 0, 0]
        past[leg][1, :, inner:] = mats[leg, 0, 1]
        is_b = modes_ref[leg, 0] == 0
        last_b[leg] = jnp.where(is_b, 1, 0)
        last_c[leg] = jnp.where(is_b, 0, 1)

    def next_branch(leg, branch):
        is_b = modes_ref[leg, branch] == 0
        top = jnp.concatenate([mats[leg, branch, 0], mats[leg, branch, 1]], axis=1)
        before = past[leg][jnp.where(is_b, last_b[leg], last_c[leg])]
        past[leg][branch + 1] = dot(before, wide_of(top)).astype(jnp.bfloat16)
        last_b[leg] = jnp.where(is_b, branch + 1, last_b[leg])
        last_c[leg] = jnp.where(is_b, last_c[leg], branch + 1)

    block = lax.broadcasted_iota(jnp.int32, (stripe, inner), 1) // width

    def apply_leg(values, wide):
        product = dot(values, wide)
        swapped = []
        for m in range(peers):
            both = []
            for comp in range(2):
                taken = None
                for t in range(peers):
                    tile = product[t * stripe : (t + 1) * stripe, comp * inner : (comp + 1) * inner]
                    shift = (t - m) * width % inner
                    if shift:
                        tile = pltpu.roll(tile, shift, 1)
                    taken = tile if taken is None else jnp.where(block == t, tile, taken)
                both.append(taken)
            swapped.append(jnp.concatenate(both, axis=1))
        return jnp.concatenate(swapped, axis=0).astype(jnp.bfloat16)

    gains = []

    def scaled(top):
        top, gain = normal(top.astype(jnp.float32))
        gains.append(gain)
        return top.astype(jnp.bfloat16)

    early = min(2, legs)
    for leg in range(legs):
        start_leg(leg)
    for branch in range(1, branches):
        for leg in range(legs):
            next_branch(leg, branch)
    own.start()
    load_proj.start()
    load_groups.start()
    wides = []
    for leg in range(legs):
        top = past[leg][last_c[leg]]
        wides.append(wide_of(top if leg < early else scaled(top)))
    from_x(0)
    load_own.wait()
    last = []
    for wave in range(WAVES):
        strip = pl.ds(wave * stripe, stripe)
        for copy in first[wave * (peers - 1) : (wave + 1) * (peers - 1)]:
            copy.wait()
        if wave == WAVES - 1:
            from_x(1)
        values = jnp.concatenate(
            [
                jnp.concatenate([got[m, 0, strip, :], got[m, 1, strip, :]], axis=1)
                for m in range(peers)
            ],
            axis=0,
        )
        for leg in range(legs):
            values = apply_leg(values, wides[leg])
        for m in range(peers):
            leave[m, strip, :] = values[m * stripe : (m + 1) * stripe]
        for step in range(1, peers):
            target = lax.rem(me + step, peers)
            copy = pltpu.make_async_remote_copy(
                src_ref=leave.at[target, strip, :],
                dst_ref=back.at[me, strip, :],
                send_sem=last_send.at[wave, step - 1],
                recv_sem=last_recv.at[wave, step - 1],
                device_id={"modes": target},
                device_id_type=MESH,
            )
            copy.start()
            last.append(copy)
    from_x(2)
    back[me] = leave[me]

    factors = [past[leg][last_b[leg]] for leg in range(legs)]
    while len(factors) > 1:
        pairs = [
            scaled(dot(factors[i], wide_of(factors[i + 1]))) for i in range(0, len(factors) - 1, 2)
        ]
        factors = pairs + factors[len(pairs) * 2 :]
    total = factors[0]
    stacked = jnp.concatenate([total[:, :inner], total[:, inner:]], axis=0)
    quad = depth // inner
    short = inner // quad
    target_row = lax.broadcasted_iota(jnp.int32, (inner, inner), 0)
    source_col = lax.broadcasted_iota(jnp.int32, (inner, inner), 1)
    order = (source_col % quad) * short + source_col // quad == target_row
    order = jnp.where(order, 1.0, 0.0).astype(jnp.bfloat16)
    turned = lax.dot_general(
        order, stacked, (((1,), (1,)), ((), ())), preferred_element_type=jnp.float32
    ).astype(jnp.bfloat16)
    real_part, imag_part = turned[:, :inner], turned[:, inner:]
    left = jnp.concatenate(
        [
            jnp.concatenate([real_part, -imag_part], axis=1),
            jnp.concatenate([imag_part, real_part], axis=1),
        ],
        axis=0,
    )
    from_y(0)
    from_x(3)
    from_y(1)

    for copy in last:
        copy.wait()
    arrived = jnp.concatenate([back[m] for m in range(peers)], axis=0)
    right = jnp.concatenate(
        [
            jnp.concatenate(
                [
                    arrived[s * inner : (s + 1) * inner, comp * inner : (comp + 1) * inner]
                    for s in range(slabs)
                ],
                axis=1,
            )
            for comp in range(2)
        ],
        axis=0,
    )
    final = dot(left, right).astype(jnp.bfloat16)
    rows = jnp.concatenate(
        [
            jnp.concatenate(
                [
                    final[
                        comp * inner + q * short : comp * inner + (q + 1) * short,
                        s * inner : (s + 1) * inner,
                    ]
                    for q in range(quad)
                ],
                axis=1,
            )
            for comp in range(2)
            for s in range(slabs)
        ],
        axis=0,
    )
    count = slabs * short
    load_groups.wait()
    spread = jnp.broadcast_to(groups_ref[...].astype(jnp.float32), (count, count))
    on_diagonal = lax.broadcasted_iota(jnp.int32, (count, count), 0)
    on_diagonal = on_diagonal == lax.broadcasted_iota(jnp.int32, (count, count), 1)
    named = jnp.sum(jnp.where(on_diagonal, spread, 0.0), axis=1, keepdims=True)
    real_sum = jnp.zeros(out_ref.shape[1:], jnp.float32)
    imag_sum = jnp.zeros(out_ref.shape[1:], jnp.float32)

    def project(group, real_sum, imag_sum):
        by_real = dot(rows, weights[group, 0])
        by_imag = dot(rows, weights[group, 1])
        here = named == group.astype(jnp.float32)
        real_sum = jnp.where(here, by_real[:count] - by_imag[count:], real_sum)
        imag_sum = jnp.where(here, by_imag[:count] + by_real[count:], imag_sum)
        return real_sum, imag_sum

    from_x(4)
    from_y(2)
    load_proj.wait()
    real_sum, imag_sum = project(home, real_sum, imag_sum)
    own.wait()
    real_sum, imag_sum = project(sibling, real_sum, imag_sum)
    real_sum, imag_sum = project(across, real_sum, imag_sum)
    for copy in over_core:
        copy.wait()
    real_sum, imag_sum = project(across_sibling, real_sum, imag_sum)
    for gain in [jnp.minimum(g, 1.0) for g in gains] + [jnp.maximum(g, 1.0) for g in gains]:
        real_sum = real_sum * gain
        imag_sum = imag_sum * gain
    out_ref[0] = real_sum.astype(jnp.bfloat16)
    out_ref[1] = imag_sum.astype(jnp.bfloat16)
    for copy in over_x:
        copy.wait_send()
    for copy in over_y:
        copy.wait_send()


def local(stem_state, branch_mats, branch_modes, out_proj, groups):
    slabs, inner = stem_state.shape[3], stem_state.shape[4]
    legs, branches = branch_mats.shape[:2]
    depth, out_len = out_proj.shape[2:]
    peers = lax.axis_size("modes")
    rows = slabs * inner
    row_total = rows * inner // depth
    part = rows // peers
    bf16 = jnp.bfloat16
    whole = pl.BlockSpec(memory_space=pl.ANY)
    result = pl.pallas_call(
        functools.partial(fused, (peers, legs, branches, slabs, inner, depth)),
        out_shape=jax.ShapeDtypeStruct((2, row_total, out_len), bf16),
        in_specs=[
            whole,
            whole,
            whole,
            whole,
            whole,
        ],
        out_specs=pl.BlockSpec(memory_space=pltpu.VMEM),
        scratch_shapes=[
            pltpu.SMEM(branch_modes.shape, jnp.int32),
            pltpu.VMEM((1, row_total), jnp.int32),
            pltpu.VMEM(branch_mats.shape, bf16),
            [pltpu.VMEM((branches + 1, inner, 2 * inner), bf16)] * legs,
            pltpu.VMEM((peers, 2, part, inner), bf16),
            pltpu.VMEM((peers, part, 2 * inner), bf16),
            pltpu.VMEM((peers, part, 2 * inner), bf16),
            pltpu.VMEM((lax.axis_size("half"), 2, depth, out_len), bf16),
            pltpu.SemaphoreType.DMA((4 + legs,)),
            pltpu.SemaphoreType.DMA((WAVES, peers - 1)),
            pltpu.SemaphoreType.DMA((WAVES, peers - 1)),
            pltpu.SemaphoreType.DMA((WAVES, peers - 1)),
            pltpu.SemaphoreType.DMA((WAVES, peers - 1)),
            pltpu.SemaphoreType.DMA((DIRECT,)),
            pltpu.SemaphoreType.DMA((DIRECT,)),
            pltpu.SemaphoreType.DMA((CHUNKS - DIRECT,)),
            pltpu.SemaphoreType.DMA((CHUNKS - DIRECT,)),
            pltpu.SemaphoreType.DMA((1 + CHUNKS,)),
            pltpu.SemaphoreType.DMA((1 + CHUNKS,)),
        ],
        compiler_params=pltpu.CompilerParams(
            collective_id=0, has_side_effects=True, vmem_limit_bytes=60 * 1024 * 1024
        ),
    )(
        stem_state.reshape(2, rows, inner),
        branch_mats,
        branch_modes,
        out_proj.reshape(out_proj.shape[1:]),
        groups.reshape(1, row_total),
    )
    return result.reshape(1, 1, 2, row_total, out_len)


def solution(mesh):
    placed = (
        P(None, ("slices", "modes"), "half", None, None, None),
        P(),
        P(),
        P("half", None, None, None),
        P(("slices", "modes"), "half", None, None),
    )
    sizes = dict(mesh.shape)
    in_kernel = sizes["half"] == 4 and sizes["slices"] == 2 and sizes["modes"] <= 4
    return jax.shard_map(
        local if in_kernel else stepwise,
        mesh=mesh,
        in_specs=placed,
        out_specs=P(("slices", "modes"), "half", None, None, None),
        check_vma=False,
    )
```
